512 devices in a mesh: row: 16 (over z), col: 16 (over y, x_hi, core), layer: 2 (over x_lo).
Axes of the slice: x: 4 (x_hi: 2, x_lo: 2; x = x_hi * 2 + x_lo), y: 4, z: 16, core: 2. Of those that a mesh axis runs over, the one named last changes fastest.
Arguments:
- left_values: float32 [6144, 6144], P('row', 'col'), may hold values from -6 to 6
- left_mask: int32 [48, 48], P('row', 'col'), may hold values from 0 to 1, as said below
- right_values: float32 [6144, 6144], P('row', 'col'), may hold values from -0.125 to 0.125
- right_mask: int32 [48, 48], P('row', 'col'), may hold values from 0 to 1, as said below
- keep_mask: int32 [48, 48], P('row', 'col'), may hold values from 0 to 1, as said below
Outputs:
- product: float32 [6144, 6144], P(('row', 'layer'), 'col')
The draws below stay inside these ranges and needn't reach their ends.
Inputs may be any that keep to these rules, and one draw needn't show every extreme that they name: `left_mask`: 0 or 1; every diagonal block is stored; the share of stored blocks differs from block row to block row. `right_mask`: 0 or 1; every diagonal block is stored; the share of stored blocks differs from block column to block column. `keep_mask`: 0 or 1; every diagonal block is retained.
All inputs are finite; a program needn't handle non-finite values.
Results may differ from the reference program's by a relative error of at most 0.00007.
Values sent between devices are 32-bit elements; how exact they have to be, the bound alone decides.
No kernel may reach another device: no remote copies, remote signals or barrier semaphores. Data moves between devices by JAX's collectives and lax.ppermute only.
A program may use at most 128 MiB of HBM per device.

```python
import jax
import jax.numpy as jnp
from jax import lax

BLK = 128
NB = 48
ORDER = 6144


def draw_left_mask(key, part):
    key = jax.random.fold_in(key, 11)
    first, second = jax.random.split(key)
    density = jax.random.randint(first, (NB, 1), 5, 61)
    rolls = jax.random.randint(second, (NB, NB), 0, 100)
    diagonal = jnp.eye(NB, dtype=jnp.int32)
    return jnp.maximum((rolls < density).astype(jnp.int32), diagonal)


def draw_right_mask(key, part):
    key = jax.random.fold_in(key, 23)
    first, second = jax.random.split(key)
    density = jax.random.randint(first, (1, NB), 5, 61)
    rolls = jax.random.randint(second, (NB, NB), 0, 100)
    diagonal = jnp.eye(NB, dtype=jnp.int32)
    return jnp.maximum((rolls < density).astype(jnp.int32), diagonal)


def draw_keep_mask(key, part):
    key = jax.random.fold_in(key, 37)
    rolls = jax.random.randint(key, (NB, NB), 0, 100)
    diagonal = jnp.eye(NB, dtype=jnp.int32)
    return jnp.maximum((rolls < 67).astype(jnp.int32), diagonal)


def block_scale(stream_key, shape, shards, smallest, top_value):
    level, own = 1.0, jax.random.fold_in(stream_key, 6)
    for dim, blocks in shards:
        draws = jnp.exp(jax.random.uniform(jax.random.fold_in(own, dim), (blocks,), jnp.float32, smallest / len(shards), top_value / len(shards)))
        level = level * jnp.repeat(draws, shape[dim] // blocks).reshape([-1 if axis == dim else 1 for axis in range(len(shape))])
    return level


def scatter_about(own_key, shape, scale, reach, cuts=(), kind=jnp.bfloat16):
    result = scale * jax.random.normal(own_key, shape, jnp.float32)
    if cuts:
        result = result * block_scale(own_key, shape, cuts, -0.22, 0.18)
    return jnp.clip(result, -reach, reach).astype(kind)


def setup_inputs(seed: int = 0) -> dict:
    keys = jax.random.split(jax.random.key(seed), 6)
    return {
        "left_values": scatter_about(keys[0], (ORDER, ORDER), 1.0, 6.0, ((0, 16), (1, 16)), jnp.float32),
        "left_mask": draw_left_mask(jax.random.fold_in(keys[5], 71), 0),
        "right_values": scatter_about(keys[2], (ORDER, ORDER), (BLK * NB // 3) ** -0.5, 0.125, ((0, 16), (1, 16)), jnp.float32),
        "right_mask": draw_right_mask(jax.random.fold_in(keys[5], 71), 0),
        "keep_mask": draw_keep_mask(jax.random.fold_in(keys[5], 71), 0),
    }


def spread(mask):
    return jnp.repeat(jnp.repeat(mask, BLK, 0), BLK, 1).astype(jnp.float32)


def reference(left_values, left_mask, right_values, right_mask, keep_mask):
    left = left_values * spread(left_mask)
    right = right_values * spread(right_mask)
    full = jnp.dot(left, right, preferred_element_type=jnp.float32, precision=lax.Precision.HIGHEST)
    return full * spread(keep_mask)
```

```python
import functools

import jax
import jax.numpy as jnp
from jax import lax
from jax.experimental import pallas as pl
from jax.experimental.pallas import tpu as pltpu
from jax.sharding import PartitionSpec as P

BLK = 128
HALF = 64
TILE = 3 * BLK
PART = TILE // 2
F32 = jnp.float32
BF16 = jnp.bfloat16
VMEM = pl.BlockSpec(memory_space=pltpu.VMEM)
SMEM = pl.BlockSpec(memory_space=pltpu.SMEM)


def call(kernel, out_shapes, in_specs, scratch=(), flops=0, nbytes=0):
    return pl.pallas_call(
        kernel,
        out_shape=out_shapes,
        in_specs=in_specs,
        out_specs=jax.tree.map(lambda _: VMEM, out_shapes),
        scratch_shapes=scratch,
        compiler_params=pltpu.CompilerParams(vmem_limit_bytes=40 * 2**20),
        cost_estimate=pl.CostEstimate(flops=flops, bytes_accessed=nbytes, transcendentals=0),
    )


def swap_halves(value):
    return pltpu.roll(value, HALF, 1)


def low_lanes(shape):
    return lax.broadcasted_iota(jnp.int32, shape, 1) < HALF


def prep_kernel(place, left_mask, right_mask, left, right, left_out, right_out):
    layer = place[2]

    def masked(values, mask, p, q, rows=slice(0, BLK)):
        block = values[p * BLK + rows.start : p * BLK + rows.stop, q * BLK : (q + 1) * BLK]
        return block * mask[p, q].astype(F32)

    def side(outer, near):
        for p in range(3):
            left_out[p * BLK : (p + 1) * BLK, :] = masked(left, left_mask, p, outer)
        middle = jnp.concatenate([masked(left, left_mask, p, 1) for p in range(3)], 0)
        top, bottom = middle[:PART], middle[PART:]
        keep_low = low_lanes((PART, BLK))
        if near == 0:
            left_out[TILE:, :] = jnp.where(keep_low, top, swap_halves(bottom))
        else:
            left_out[TILE:, :] = jnp.where(keep_low, swap_halves(top), bottom)
        rows = slice(near * HALF, (near + 1) * HALF)
        for q in range(3):
            lanes = slice(q * BLK, (q + 1) * BLK)
            right_out[:BLK, lanes] = masked(right, right_mask, outer, q)
            right_out[BLK:, lanes] = masked(right, right_mask, 1, q, rows)

    @pl.when(layer == 0)
    def _():
        side(0, 0)

    @pl.when(layer == 1)
    def _():
        side(2, 1)


def split(value):
    high = value.astype(BF16)
    return high, (value - high.astype(F32)).astype(BF16)


def triple(left, right):
    (lh, ll), (rh, rl) = left, right
    dot = functools.partial(jnp.dot, preferred_element_type=F32)
    return dot(lh, rh) + (dot(lh, rl) + dot(ll, rh))


def join_left(one, two):
    m1, m2 = one[TILE:], two[TILE:]
    keep_low = low_lanes((PART, BLK))
    top = jnp.where(keep_low, m1, swap_halves(m2))
    bottom = jnp.where(keep_low, swap_halves(m1), m2)
    return jnp.concatenate([one[:TILE], two[:TILE], jnp.concatenate([top, bottom], 0)], 1)


def join_right(one, two):
    return jnp.concatenate([one[:BLK], two[:BLK], one[BLK:], two[BLK:]], 0)


def panel_index(place, k):
    col = place[1]
    return lax.rem(k, 2) == lax.rem(col, 2), k // 4, lax.bitwise_xor(lax.rem(k // 2, 2), lax.rem(col // 2, 2))


def fill(place, same, other, step, rights, lh, ll, rh, rl, column):
    z = place[0]
    behind, ahead = lax.rem(z - step + 16, 16), lax.rem(z + step, 16)
    mine, y1, x1 = panel_index(place, behind)
    _, y2, x2 = panel_index(place, ahead)
    span = slice(column, column + TILE)

    def put(panel):
        one, two = panel[y1, x1], panel[y2, x2]
        if step == 0:
            two = jnp.zeros_like(two)
        lh[:, span], ll[:, span] = split(join_left(one, two))

    pl.when(mine)(lambda: put(same))
    pl.when(jnp.logical_not(mine))(lambda: put(other))
    one = rights[0][...]
    two = jnp.zeros_like(one) if step == 0 else rights[1][...]
    rh[span, :], rl[span, :] = split(join_right(one, two))


def main_kernel(steps, place, same, other, *refs):
    rights, (total, lh, ll, rh, rl) = refs[:-5], refs[-5:]
    for number, step in enumerate(steps):
        pair = rights[:1] if step == 0 else rights[2 * step - 1 : 2 * step + 1]
        fill(place, same, other, step, pair, lh, ll, rh, rl, number * TILE)
    total[...] = triple((lh[...], ll[...]), (rh[...], rl[...]))


def near_kernel(step, place, same, other, behind, ahead, total, own, away, lh, ll, rh, rl):
    fill(place, same, other, step, (behind, ahead), lh, ll, rh, rl, 0)
    value = total[...] + triple((lh[...], ll[...]), (rh[...], rl[...]))
    layer = place[2]

    @pl.when(layer == 0)
    def _():
        own[...] = value[:PART]
        away[...] = value[PART:]

    @pl.when(layer == 1)
    def _():
        own[...] = value[PART:]
        away[...] = value[:PART]


def last_kernel(place, keep, own, came, left_own, left_other, right_own, right_other, out):
    layer = place[2]
    first = layer == 0

    def rows_of(packed):
        outer = jnp.where(first, packed[:PART], packed[PART:TILE])
        middle = jnp.where(first, packed[TILE:], swap_halves(packed[TILE:]))
        return outer, middle

    outer1, middle1 = rows_of(left_own[...])
    outer2, middle2 = rows_of(left_other[...])
    middle = jnp.where(low_lanes((PART, BLK)), middle1, swap_halves(middle2))
    left = jnp.concatenate([outer1, outer2, middle], 1)
    right = join_right(right_own[...], right_other[...])
    value = own[...] + came[...] + triple(split(left), split(right))
    for q in range(3):
        lanes = slice(q * BLK, (q + 1) * BLK)
        ends = jnp.where(first, keep[0, q], keep[2, q]).astype(F32)
        centre = keep[1, q].astype(F32)
        row = lax.broadcasted_iota(jnp.int32, (PART, BLK), 0) + layer * PART
        scale = jnp.where((row >= BLK) & (row < 2 * BLK), centre, ends)
        out[:, lanes] = value[:, lanes] * scale


def shift(value, axis, steps):
    count = lax.axis_size(axis)
    return lax.ppermute(value, axis, [(i, (i + steps) % count) for i in range(count)])


def shards(left_values, left_mask, right_values, right_mask, keep_mask):
    count = lax.axis_size("row")
    cols = lax.axis_size("col")
    z, col, layer = lax.axis_index("row"), lax.axis_index("col"), lax.axis_index("layer")
    place = jnp.stack([z, col, layer]).astype(jnp.int32)
    packed = jax.ShapeDtypeStruct((TILE + PART, BLK), F32)
    half = jax.ShapeDtypeStruct((PART, TILE), F32)
    whole = jax.ShapeDtypeStruct((TILE, TILE), F32)

    left, right = call(prep_kernel, (packed, half), [SMEM] * 3 + [VMEM] * 2)(
        place, left_mask, right_mask, left_values, right_values
    )

    left_x = lax.ppermute(left, "col", [(i, i ^ 2) for i in range(cols)])
    groups = [[j + 4 * y for y in range(4)] for j in range(4)]
    same = lax.all_gather(jnp.stack([left, left_x]), "col", axis_index_groups=groups)
    other = lax.ppermute(same, "col", [(i, i ^ 1) for i in range(cols)])

    reach = count // 2
    rights, behind, ahead = [right], right, right
    for _ in range(1, reach):
        behind, ahead = shift(behind, "row", 1), shift(ahead, "row", -1)
        rights += [behind, ahead]
    far_own = shift(behind, "row", 1)
    cross = [(z0 * 2 + l0, (z0 - 1) % count * 2 + 1 - l0) for z0 in range(count) for l0 in range(2)]
    far_other = lax.ppermute(ahead, ("row", "layer"), cross)

    def parts(n):
        return [
            pltpu.VMEM((TILE, n * TILE), BF16), pltpu.VMEM((TILE, n * TILE), BF16),
            pltpu.VMEM((n * TILE, TILE), BF16), pltpu.VMEM((n * TILE, TILE), BF16),
        ]

    steps = tuple(range(reach - 1))
    first = rights[: 2 * len(steps) - 1]
    total = call(
        functools.partial(main_kernel, steps), whole, [SMEM] + [VMEM] * (2 + len(first)), parts(len(steps)),
        flops=6 * TILE * TILE * TILE * len(steps), nbytes=10 * 2**20,
    )(place, same, other, *first)
    own, away = call(
        functools.partial(near_kernel, reach - 1), (half, half), [SMEM] + [VMEM] * 5, parts(1),
        flops=6 * TILE * TILE * TILE, nbytes=2**20,
    )(place, same, other, *rights[-2:], total)
    came = shift(away, "layer", 1)

    far = (z + reach) % count
    mine, y, x = panel_index(place, far)
    left_own = jnp.where(mine, same[y, x], other[y, x])
    left_other = shift(left_own, "layer", 1)
    return call(last_kernel, half, [SMEM] * 2 + [VMEM] * 6, flops=6 * PART * TILE * TILE, nbytes=2**20)(
        place, keep_mask, own, came, left_own, left_other, far_own, far_other
    )


def solution(mesh):
    specs = (P("row", "col"),) * 5
    return jax.shard_map(shards, mesh=mesh, in_specs=specs, out_specs=P(("row", "layer"), "col"), check_vma=False)
```

```python
import functools

import jax
import jax.numpy as jnp
from jax import lax
from jax.experimental import pallas as pl
from jax.experimental.pallas import tpu as pltpu
from jax.sharding import PartitionSpec as P

BLK = 128
HALF = 64
TILE = 3 * BLK
PART = TILE // 2
F32 = jnp.float32
BF16 = jnp.bfloat16
VMEM = pl.BlockSpec(memory_space=pltpu.VMEM)
SMEM = pl.BlockSpec(memory_space=pltpu.SMEM)


def call(kernel, out_shapes, in_specs, scratch=(), flops=0, nbytes=0):
    return pl.pallas_call(
        kernel,
        out_shape=out_shapes,
        in_specs=in_specs,
        out_specs=jax.tree.map(lambda _: VMEM, out_shapes),
        scratch_shapes=scratch,
        compiler_params=pltpu.CompilerParams(vmem_limit_bytes=20 * 2**20),
        cost_estimate=pl.CostEstimate(flops=flops, bytes_accessed=nbytes, transcendentals=0),
    )


def swap_halves(value):
    return pltpu.roll(value, HALF, 1)


def low_lanes(shape):
    return lax.broadcasted_iota(jnp.int32, shape, 1) < HALF


def prep_kernel(place, left_mask, right_mask, left, right, left_out, right_out):
    layer = place[2]

    def masked(values, mask, p, q, rows=slice(0, BLK)):
        block = values[p * BLK + rows.start : p * BLK + rows.stop, q * BLK : (q + 1) * BLK]
        return block * mask[p, q].astype(F32)

    def side(outer, near):
        for p in range(3):
            left_out[p * BLK : (p + 1) * BLK, :] = masked(left, left_mask, p, outer)
        middle = jnp.concatenate([masked(left, left_mask, p, 1) for p in range(3)], 0)
        top, bottom = middle[:PART], middle[PART:]
        keep_low = low_lanes((PART, BLK))
        if near == 0:
            left_out[TILE:, :] = jnp.where(keep_low, top, swap_halves(bottom))
        else:
            left_out[TILE:, :] = jnp.where(keep_low, swap_halves(top), bottom)
        rows = slice(near * HALF, (near + 1) * HALF)
        for q in range(3):
            lanes = slice(q * BLK, (q + 1) * BLK)
            right_out[:BLK, lanes] = masked(right, right_mask, outer, q)
            right_out[BLK:, lanes] = masked(right, right_mask, 1, q, rows)

    @pl.when(layer == 0)
    def _():
        side(0, 0)

    @pl.when(layer == 1)
    def _():
        side(2, 1)


def split(value):
    high = value.astype(BF16)
    return high, (value - high.astype(F32)).astype(BF16)


def triple(left, right):
    (lh, ll), (rh, rl) = left, right
    dot = functools.partial(jnp.dot, preferred_element_type=F32)
    return dot(lh, rh) + (dot(lh, rl) + dot(ll, rh))


def join_left(one, two):
    m1, m2 = one[TILE:], two[TILE:]
    keep_low = low_lanes((PART, BLK))
    top = jnp.where(keep_low, m1, swap_halves(m2))
    bottom = jnp.where(keep_low, swap_halves(m1), m2)
    return jnp.concatenate([one[:TILE], two[:TILE], jnp.concatenate([top, bottom], 0)], 1)


def join_right(one, two):
    return jnp.concatenate([one[:BLK], two[:BLK], one[BLK:], two[BLK:]], 0)


def panel_index(place, k):
    col = place[1]
    return lax.rem(k, 2) == lax.rem(col, 2), k // 4, lax.bitwise_xor(lax.rem(k // 2, 2), lax.rem(col // 2, 2))


def fill(place, same, other, step, rights, lh, ll, rh, rl, column):
    z = place[0]
    behind, ahead = lax.rem(z - step + 16, 16), lax.rem(z + step, 16)
    mine, y1, x1 = panel_index(place, behind)
    _, y2, x2 = panel_index(place, ahead)
    span = slice(column, column + TILE)

    def put(panel):
        one, two = panel[y1, x1], panel[y2, x2]
        if step == 0:
            two = jnp.zeros_like(two)
        lh[:, span], ll[:, span] = split(join_left(one, two))

    pl.when(mine)(lambda: put(same))
    pl.when(jnp.logical_not(mine))(lambda: put(other))
    one = rights[0][...]
    two = jnp.zeros_like(one) if step == 0 else rights[1][...]
    rh[span, :], rl[span, :] = split(join_right(one, two))


def main_kernel(steps, place, same, other, *refs):
    rights, (total, lh, ll, rh, rl) = refs[:-5], refs[-5:]
    for number, step in enumerate(steps):
        pair = rights[:1] if step == 0 else rights[2 * step - 1 : 2 * step + 1]
        fill(place, same, other, step, pair, lh, ll, rh, rl, number * TILE)
    total[...] = triple((lh[...], ll[...]), (rh[...], rl[...]))


def near_kernel(steps, place, same, other, *refs):
    rights, (total, own, away, lh, ll, rh, rl) = refs[:-7], refs[-7:]
    for number, step in enumerate(steps):
        fill(place, same, other, step, rights[2 * number : 2 * number + 2], lh, ll, rh, rl, number * TILE)
    value = total[...] + triple((lh[...], ll[...]), (rh[...], rl[...]))
    layer = place[2]

    @pl.when(layer == 0)
    def _():
        own[...] = value[:PART]
        away[...] = value[PART:]

    @pl.when(layer == 1)
    def _():
        own[...] = value[PART:]
        away[...] = value[:PART]


def last_kernel(place, keep, own, came, left_own, left_other, right_own, right_other, out):
    layer = place[2]
    first = layer == 0

    def rows_of(packed):
        outer = jnp.where(first, packed[:PART], packed[PART:TILE])
        middle = jnp.where(first, packed[TILE:], swap_halves(packed[TILE:]))
        return outer, middle

    outer1, middle1 = rows_of(left_own[...])
    outer2, middle2 = rows_of(left_other[...])
    middle = jnp.where(low_lanes((PART, BLK)), middle1, swap_halves(middle2))
    left = jnp.concatenate([outer1, outer2, middle], 1)
    right = join_right(right_own[...], right_other[...])
    value = own[...] + came[...] + triple(split(left), split(right))
    for q in range(3):
        lanes = slice(q * BLK, (q + 1) * BLK)
        ends = jnp.where(first, keep[0, q], keep[2, q]).astype(F32)
        centre = keep[1, q].astype(F32)
        row = lax.broadcasted_iota(jnp.int32, (PART, BLK), 0) + layer * PART
        scale = jnp.where((row >= BLK) & (row < 2 * BLK), centre, ends)
        out[:, lanes] = value[:, lanes] * scale


def shift(value, axis, steps):
    count = lax.axis_size(axis)
    return lax.ppermute(value, axis, [(i, (i + steps) % count) for i in range(count)])


def after(value, *earlier):
    return lax.optimization_barrier((value, *earlier))[0]


def shards(left_values, left_mask, right_values, right_mask, keep_mask):
    count = lax.axis_size("row")
    cols = lax.axis_size("col")
    z, col, layer = lax.axis_index("row"), lax.axis_index("col"), lax.axis_index("layer")
    place = jnp.stack([z, col, layer]).astype(jnp.int32)
    packed = jax.ShapeDtypeStruct((TILE + PART, BLK), F32)
    half = jax.ShapeDtypeStruct((PART, TILE), F32)
    whole = jax.ShapeDtypeStruct((TILE, TILE), F32)

    left, right = call(prep_kernel, (packed, half), [SMEM] * 3 + [VMEM] * 2)(
        place, left_mask, right_mask, left_values, right_values
    )

    left_x = lax.ppermute(left, "col", [(i, i ^ 2) for i in range(cols)])
    groups = [[j + 4 * y for y in range(4)] for j in range(4)]
    same = lax.all_gather(jnp.stack([left, left_x]), "col", axis_index_groups=groups)

    def parts(n):
        return [
            pltpu.VMEM((TILE, n * TILE), BF16), pltpu.VMEM((TILE, n * TILE), BF16),
            pltpu.VMEM((n * TILE, TILE), BF16), pltpu.VMEM((n * TILE, TILE), BF16),
        ]

    reach = count // 2
    rights, behind, ahead = [right], right, right
    for step in range(1, reach):
        if step == reach - 1:
            steps = tuple(range(reach - 2))
            first = rights[: 2 * len(steps) - 1]
            total = call(
                functools.partial(main_kernel, steps), whole, [SMEM] + [VMEM] * (2 + len(first)), parts(len(steps)),
                flops=6 * TILE * TILE * TILE * len(steps), nbytes=10 * 2**20,
            )(place, same, other, *first)
            far = (z + reach) % count
            mine, y, x = panel_index(place, far)
            left_own = jnp.where(mine, same[y, x], other[y, x])
            left_other = shift(left_own, "layer", 1)
            behind, ahead = after(behind, total, left_other), after(ahead, total, left_other)
        behind, ahead = shift(behind, "row", 1), shift(ahead, "row", -1)
        rights += [behind, ahead]
        if step == reach - 3:
            same = after(same, behind, ahead)
            other = lax.ppermute(same, "col", [(i, i ^ 1) for i in range(cols)])
    own, away = call(
        functools.partial(near_kernel, (reach - 2, reach - 1)), (half, half), [SMEM] + [VMEM] * 7, parts(2),
        flops=6 * TILE * TILE * TILE, nbytes=2**20,
    )(place, same, other, *rights[-4:], total)
    came = shift(away, "layer", 1)
    behind, ahead = after(behind, away), after(ahead, away)
    far_own = shift(behind, "row", 1)
    cross = [(z0 * 2 + l0, (z0 - 1) % count * 2 + 1 - l0) for z0 in range(count) for l0 in range(2)]
    far_other = lax.ppermute(ahead, ("row", "layer"), cross)
    return call(last_kernel, half, [SMEM] * 2 + [VMEM] * 6, flops=6 * PART * TILE * TILE, nbytes=2**20)(
        place, keep_mask, own, came, left_own, left_other, far_own, far_other
    )


def solution(mesh):
    specs = (P("row", "col"),) * 5
    return jax.shard_map(shards, mesh=mesh, in_specs=specs, out_specs=P(("row", "layer"), "col"), check_vma=False)
```

```python
import functools

import jax
import jax.numpy as jnp
from jax import lax
from jax.experimental import pallas as pl
from jax.experimental.pallas import tpu as pltpu
from jax.sharding import PartitionSpec as P

BLK = 128
HALF = 64
TILE = 3 * BLK
PART = TILE // 2
F32 = jnp.float32
BF16 = jnp.bfloat16
VMEM = pl.BlockSpec(memory_space=pltpu.VMEM)
SMEM = pl.BlockSpec(memory_space=pltpu.SMEM)
ANY = pl.BlockSpec(memory_space=pl.ANY)
LIMIT = 20 * 2**20


def call(kernel, out_shapes, in_specs, scratch=(), flops=0, nbytes=0):
    return pl.pallas_call(
        kernel,
        out_shape=out_shapes,
        in_specs=in_specs,
        out_specs=jax.tree.map(lambda _: VMEM, out_shapes),
        scratch_shapes=scratch,
        compiler_params=pltpu.CompilerParams(vmem_limit_bytes=LIMIT),
        cost_estimate=pl.CostEstimate(flops=flops, bytes_accessed=nbytes, transcendentals=0),
    )


def swap_halves(value):
    return pltpu.roll(value, HALF, 1)


def low_lanes(shape):
    return lax.broadcasted_iota(jnp.int32, shape, 1) < HALF


def fetch(pairs, sems):
    copies = [pltpu.make_async_copy(src, dst, sems.at[i]) for i, (src, dst) in enumerate(pairs)]
    for copy in copies:
        copy.start()
    return copies


def masked(values, mask, p, q, rows=slice(0, BLK)):
    block = values[p * BLK + rows.start : p * BLK + rows.stop, q * BLK : (q + 1) * BLK]
    return block * mask[p : p + 1, q : q + 1].astype(F32)


def prep_kernel(place, lm_in, rm_in, left_in, right_in, left_out, right_out, lm, rm, left, right, sems):
    z, col, layer = place[0], place[1], place[2]
    for copy in fetch(((rm_in, rm), (right_in, right), (lm_in, lm), (left_in, left)), sems):
        copy.wait()
    far = lax.rem(z + 8, 16) == col

    def right_side(outer, near):
        rows = slice(near * HALF, (near + 1) * HALF)
        for q in range(3):
            lanes = slice(q * BLK, (q + 1) * BLK)
            right_out[:BLK, lanes] = masked(right, rm, outer, q)
            right_out[BLK:, lanes] = masked(right, rm, 1, q, rows)

    def left_side(outer, near):
        for p in range(3):
            left_out[p * BLK : (p + 1) * BLK, :] = masked(left, lm, p, outer)
        middle = jnp.concatenate([masked(left, lm, p, 1) for p in range(3)], 0)
        top, bottom = middle[:PART], middle[PART:]
        keep_low = low_lanes((PART, BLK))
        if near == 0:
            left_out[TILE:, :] = jnp.where(keep_low, top, swap_halves(bottom))
        else:
            left_out[TILE:, :] = jnp.where(keep_low, swap_halves(top), bottom)

    def left_far(outer, near):
        for q in range(3):
            start = q * PART
            end = masked(left, lm, outer, q)
            mid = masked(left, lm, 1, q, slice(near * HALF, (near + 1) * HALF))
            left_out[start : start + PART, :] = jnp.concatenate([end, mid] if near == 0 else [mid, end], 0)

    for side in (0, 1):

        @pl.when(layer == side)
        def _(outer=2 * side, near=side):
            right_side(outer, near)
            pl.when(far)(lambda: left_far(outer, near))
            pl.when(jnp.logical_not(far))(lambda: left_side(outer, near))


def split(value):
    high = value.astype(BF16)
    return high, (value - high.astype(F32)).astype(BF16)


def triple(left, right):
    (lh, ll), (rh, rl) = left, right
    dot = functools.partial(jnp.dot, preferred_element_type=F32)
    return dot(lh, rh) + (dot(lh, rl) + dot(ll, rh))


def join_left(one, two):
    m1, m2 = one[TILE:], two[TILE:]
    keep_low = low_lanes((PART, BLK))
    top = jnp.where(keep_low, m1, swap_halves(m2))
    bottom = jnp.where(keep_low, swap_halves(m1), m2)
    return jnp.concatenate([one[:TILE], two[:TILE], jnp.concatenate([top, bottom], 0)], 1)


def join_right(one, two):
    return jnp.concatenate([one[:BLK], two[:BLK], one[BLK:], two[BLK:]], 0)


def panel_index(place, k):
    col = place[1]
    mine = lax.rem(k, 2) == lax.rem(col, 2)
    return mine, lax.rem(col // 4 - k // 4 + 4, 4), lax.bitwise_xor(lax.rem(k // 2, 2), lax.rem(col // 2, 2))


def fill_left(place, same, other, step, lh, ll, column):
    z = place[0]
    mine, y1, x1 = panel_index(place, lax.rem(z - step + 16, 16))
    _, y2, x2 = panel_index(place, lax.rem(z + step, 16))
    span = slice(column, column + TILE)

    def put(panel):
        one, two = panel[y1, x1], panel[y2, x2]
        if step == 0:
            two = jnp.zeros_like(two)
        lh[:, span], ll[:, span] = split(join_left(one, two))

    pl.when(mine)(lambda: put(same))
    pl.when(jnp.logical_not(mine))(lambda: put(other))


def fill_right(one, two, rh, rl, column):
    span = slice(column, column + TILE)
    rh[span, :], rl[span, :] = split(join_right(one, two))


def main_kernel(early, late, place, same_in, other_in, *refs):
    n = 2 * len(early) - 1
    rights_in, (total, far, late_h, late_l, same, other, rights, lh, ll, rh, rl, sems) = refs[:n], refs[n:]
    pairs = [(same_in, same), (other_in, other)] + [(rights_in[i], rights.at[i]) for i in range(n)]
    copies = fetch(pairs, sems)
    copies[0].wait()
    copies[1].wait()
    for number, step in enumerate(early):
        fill_left(place, same, other, step, lh, ll, number * TILE)
    for number, step in enumerate(early):
        if step == 0:
            copies[2].wait()
            one, two = rights[0], jnp.zeros((PART, TILE), F32)
        else:
            copies[2 * step + 1].wait()
            copies[2 * step + 2].wait()
            one, two = rights[2 * step - 1], rights[2 * step]
        fill_right(one, two, rh, rl, number * TILE)
    total[...] = triple((lh[...], ll[...]), (rh[...], rl[...]))
    for number, step in enumerate(late):
        fill_left(place, same, other, step, late_h, late_l, number * TILE)
    mine, y, x = panel_index(place, lax.rem(place[0] + 8, 16))

    @pl.when(mine)
    def _():
        far[...] = same[y, x]

    @pl.when(jnp.logical_not(mine))
    def _():
        far[...] = other[y, x]


def near_kernel(place, total, late_h, late_l, *refs):
    rights, (own, away, rh, rl) = refs[:-4], refs[-4:]
    for number in range(len(rights) // 2):
        fill_right(rights[2 * number][...], rights[2 * number + 1][...], rh, rl, number * TILE)
    value = total[...] + triple((late_h[...], late_l[...]), (rh[...], rl[...]))
    layer = place[2]

    @pl.when(layer == 0)
    def _():
        own[...] = value[:PART]
        away[...] = value[PART:]

    @pl.when(layer == 1)
    def _():
        own[...] = value[PART:]
        away[...] = value[:PART]


def last_kernel(place, keep, own, came, far, right_own, right_other, out):
    layer = place[2]
    first = layer == 0
    mine, other = right_own[...], right_other[...]
    low, high = jnp.where(first, mine, other), jnp.where(first, other, mine)
    right = jnp.concatenate([low, high[BLK:], high[:BLK]], 0)
    left = jnp.concatenate([far[:PART], far[PART : 2 * PART], far[2 * PART :]], 1)
    value = own[...] + came[...] + triple(split(left), split(right))
    row = lax.broadcasted_iota(jnp.int32, (PART, BLK), 0) + layer * PART
    centre = (row >= BLK) & (row < 2 * BLK)
    for q in range(3):
        lanes = slice(q * BLK, (q + 1) * BLK)
        ends = jnp.where(first, keep[0:1, q : q + 1], keep[2:3, q : q + 1]).astype(F32)
        scale = jnp.where(centre, keep[1:2, q : q + 1].astype(F32), ends)
        out[:, lanes] = value[:, lanes] * scale


def shift(value, axis, steps):
    count = lax.axis_size(axis)
    return lax.ppermute(value, axis, [(i, (i + steps) % count) for i in range(count)])


def after(value, *earlier):
    return lax.optimization_barrier((value, *earlier))[0]


def shards(left_values, left_mask, right_values, right_mask, keep_mask):
    count = lax.axis_size("row")
    cols = lax.axis_size("col")
    z, col, layer = lax.axis_index("row"), lax.axis_index("col"), lax.axis_index("layer")
    place = jnp.stack([z, col, layer]).astype(jnp.int32)
    packed = jax.ShapeDtypeStruct((TILE + PART, BLK), F32)
    half = jax.ShapeDtypeStruct((PART, TILE), F32)
    whole = jax.ShapeDtypeStruct((TILE, TILE), F32)
    mask = pltpu.VMEM((3, 3), jnp.int32)

    left, right = call(
        prep_kernel, (packed, half), [SMEM] + [ANY] * 4,
        [mask, mask, pltpu.VMEM((TILE, TILE), F32), pltpu.VMEM((TILE, TILE), F32), pltpu.SemaphoreType.DMA((4,))],
        nbytes=2**21,
    )(place, left_mask, right_mask, left_values, right_values)

    left_x = lax.ppermute(left, "col", [(i, i ^ 2) for i in range(cols)])
    pair = jnp.stack([left, left_x])
    pieces = [pair]

    reach = count // 2
    early, late = tuple(range(reach - 2)), (reach - 2, reach - 1)
    rights, behind, ahead = [right], right, right
    for step in range(1, reach):
        if step > 1:
            behind, ahead = after(behind, rights[2 * step - 4]), after(ahead, behind)
        behind, ahead = shift(behind, "row", 1), shift(ahead, "row", -1)
        rights += [behind, ahead]
        if step <= 3:
            pair = after(pair, behind)
            pieces.append(lax.ppermute(pair, "col", [(i, (i + 4 * step) % cols) for i in range(cols)]))
        if step == reach - 3:
            same = after(jnp.stack(pieces), behind)
            other = lax.ppermute(same, "col", [(i, i ^ 1) for i in range(cols)])

    n = 2 * len(early) - 1
    panel = pltpu.VMEM((4, 2, TILE + PART, BLK), F32)
    part = jax.ShapeDtypeStruct((TILE, len(late) * TILE), BF16)
    lefts, downs = pltpu.VMEM((TILE, len(early) * TILE), BF16), pltpu.VMEM((len(early) * TILE, TILE), BF16)
    total, far, late_h, late_l = call(
        functools.partial(main_kernel, early, late), (whole, packed, part, part), [SMEM] + [ANY] * (2 + n),
        [panel, panel, pltpu.VMEM((n, PART, TILE), F32), lefts, lefts, downs, downs, pltpu.SemaphoreType.DMA((2 + n,))],
        flops=6 * TILE**3 * len(early), nbytes=10 * 2**20,
    )(place, same, other, *rights[:n])
    downs = pltpu.VMEM((len(late) * TILE, TILE), BF16)
    own, away = call(
        near_kernel, (half, half), [SMEM] + [VMEM] * (3 + 2 * len(late)), [downs, downs],
        flops=6 * TILE**3 * len(late), nbytes=2**21,
    )(place, total, late_h, late_l, *rights[n:])
    came = shift(away, "layer", 1)
    behind, ahead = after(behind, away), after(ahead, away)
    far_own = shift(behind, "row", 1)
    cross = [(z0 * 2 + l0, (z0 - 1) % count * 2 + 1 - l0) for z0 in range(count) for l0 in range(2)]
    far_other = lax.ppermute(ahead, ("row", "layer"), cross)
    return call(last_kernel, half, [SMEM] + [VMEM] * 6, flops=6 * PART * TILE * TILE, nbytes=2**20)(
        place, keep_mask, own, came, far, far_own, far_other
    )


def solution(mesh):
    specs = (P("row", "col"),) * 5
    return jax.shard_map(shards, mesh=mesh, in_specs=specs, out_specs=P(("row", "layer"), "col"), check_vma=False)
```

```python
import functools

import jax
import jax.numpy as jnp
from jax import lax
from jax.experimental import pallas as pl
from jax.experimental.pallas import tpu as pltpu
from jax.sharding import PartitionSpec as P

BLK = 128
HALF = 64
TILE = 3 * BLK
PART = TILE // 2
F32 = jnp.float32
BF16 = jnp.bfloat16
VMEM = pl.BlockSpec(memory_space=pltpu.VMEM)
SMEM = pl.BlockSpec(memory_space=pltpu.SMEM)
ANY = pl.BlockSpec(memory_space=pl.ANY)


def call(kernel, out_shapes, in_specs, scratch=(), flops=0, nbytes=0, limit=20):
    return pl.pallas_call(
        kernel,
        out_shape=out_shapes,
        in_specs=in_specs,
        out_specs=jax.tree.map(lambda _: VMEM, out_shapes),
        scratch_shapes=scratch,
        compiler_params=pltpu.CompilerParams(vmem_limit_bytes=limit * 2**20),
        cost_estimate=pl.CostEstimate(flops=flops, bytes_accessed=nbytes, transcendentals=0),
    )


def swap_halves(value):
    return pltpu.roll(value, HALF, 1)


def low_lanes(shape):
    return lax.broadcasted_iota(jnp.int32, shape, 1) < HALF


def fetch(pairs, sems):
    copies = [pltpu.make_async_copy(src, dst, sems.at[i]) for i, (src, dst) in enumerate(pairs)]
    for copy in copies:
        copy.start()
    return copies


def masked(values, mask, p, q, rows=slice(0, BLK)):
    block = values[p * BLK + rows.start : p * BLK + rows.stop, q * BLK : (q + 1) * BLK]
    return block * mask[p : p + 1, q : q + 1].astype(F32)


def prep_kernel(place, lm_in, rm_in, left_in, right_in, left_out, right_out, lm, rm, left, right, sems):
    z, col, layer = place[0], place[1], place[2]
    for copy in fetch(((rm_in, rm), (right_in, right), (lm_in, lm), (left_in, left)), sems):
        copy.wait()
    far = lax.rem(z + 8, 16) == col

    def right_side(outer, near):
        rows = slice(near * HALF, (near + 1) * HALF)
        for q in range(3):
            lanes = slice(q * BLK, (q + 1) * BLK)
            right_out[:BLK, lanes] = masked(right, rm, outer, q)
            right_out[BLK:, lanes] = masked(right, rm, 1, q, rows)

    def left_side(outer, near):
        for p in range(3):
            left_out[p * BLK : (p + 1) * BLK, :] = masked(left, lm, p, outer)
        middle = jnp.concatenate([masked(left, lm, p, 1) for p in range(3)], 0)
        top, bottom = middle[:PART], middle[PART:]
        keep_low = low_lanes((PART, BLK))
        if near == 0:
            left_out[TILE:, :] = jnp.where(keep_low, top, swap_halves(bottom))
        else:
            left_out[TILE:, :] = jnp.where(keep_low, swap_halves(top), bottom)

    def left_far(outer, near):
        for q in range(3):
            start = q * PART
            end = masked(left, lm, outer, q)
            mid = masked(left, lm, 1, q, slice(near * HALF, (near + 1) * HALF))
            left_out[start : start + PART, :] = jnp.concatenate([end, mid] if near == 0 else [mid, end], 0)

    for side in (0, 1):

        @pl.when(layer == side)
        def _(outer=2 * side, near=side):
            right_side(outer, near)
            pl.when(far)(lambda: left_far(outer, near))
            pl.when(jnp.logical_not(far))(lambda: left_side(outer, near))


def split(value):
    high = value.astype(BF16)
    return high, (value - high.astype(F32)).astype(BF16)


def triple(left, right):
    (lh, ll), (rh, rl) = left, right
    dot = functools.partial(jnp.dot, preferred_element_type=F32)
    return dot(lh, rh) + (dot(lh, rl) + dot(ll, rh))


def join_left(one, two):
    m1, m2 = one[TILE:], two[TILE:]
    keep_low = low_lanes((PART, BLK))
    top = jnp.where(keep_low, m1, swap_halves(m2))
    bottom = jnp.where(keep_low, swap_halves(m1), m2)
    return jnp.concatenate([one[:TILE], two[:TILE], jnp.concatenate([top, bottom], 0)], 1)


def join_right(one, two):
    return jnp.concatenate([one[:BLK], two[:BLK], one[BLK:], two[BLK:]], 0)


def panel_index(place, k):
    col = place[1]
    mine = lax.rem(k, 2) == lax.rem(col, 2)
    return mine, lax.rem(col // 4 - k // 4 + 4, 4), lax.bitwise_xor(lax.rem(k // 2, 2), lax.rem(col // 2, 2))


def fill_left(place, same, other, step, lh, ll, column):
    z = place[0]
    mine, y1, x1 = panel_index(place, lax.rem(z - step + 16, 16))
    _, y2, x2 = panel_index(place, lax.rem(z + step, 16))
    span = slice(column, column + TILE)

    def put(panel):
        one, two = panel[y1, x1], panel[y2, x2]
        if step == 0:
            two = jnp.zeros_like(two)
        lh[:, span], ll[:, span] = split(join_left(one, two))

    pl.when(mine)(lambda: put(same))
    pl.when(jnp.logical_not(mine))(lambda: put(other))


def fill_right(one, two, rh, rl, column):
    span = slice(column, column + TILE)
    rh[span, :], rl[span, :] = split(join_right(one, two))


def main_kernel(early, late, place, same, other, *refs):
    n = 2 * len(early) - 1
    rights, (total, far, late_h, late_l, lh, ll, rh, rl) = refs[:n], refs[n:]
    for number, step in enumerate(early):
        fill_left(place, same, other, step, lh, ll, number * TILE)
        one = rights[0 if step == 0 else 2 * step - 1][...]
        two = jnp.zeros_like(one) if step == 0 else rights[2 * step][...]
        fill_right(one, two, rh, rl, number * TILE)
    total[...] = triple((lh[...], ll[...]), (rh[...], rl[...]))
    for number, step in enumerate(late):
        fill_left(place, same, other, step, late_h, late_l, number * TILE)
    mine, y, x = panel_index(place, lax.rem(place[0] + 8, 16))

    @pl.when(mine)
    def _():
        far[...] = same[y, x]

    @pl.when(jnp.logical_not(mine))
    def _():
        far[...] = other[y, x]


def near_kernel(place, total, late_h, late_l, *refs):
    rights, (own, away, rh, rl) = refs[:-4], refs[-4:]
    for number in range(len(rights) // 2):
        fill_right(rights[2 * number][...], rights[2 * number + 1][...], rh, rl, number * TILE)
    value = total[...] + triple((late_h[...], late_l[...]), (rh[...], rl[...]))
    layer = place[2]

    @pl.when(layer == 0)
    def _():
        own[...] = value[:PART]
        away[...] = value[PART:]

    @pl.when(layer == 1)
    def _():
        own[...] = value[PART:]
        away[...] = value[:PART]


def last_kernel(place, keep, own, came, far, right_own, right_other, out):
    layer = place[2]
    first = layer == 0
    mine, other = right_own[...], right_other[...]
    low, high = jnp.where(first, mine, other), jnp.where(first, other, mine)
    right = jnp.concatenate([low, high[BLK:], high[:BLK]], 0)
    left = jnp.concatenate([far[:PART], far[PART : 2 * PART], far[2 * PART :]], 1)
    value = own[...] + came[...] + triple(split(left), split(right))
    row = lax.broadcasted_iota(jnp.int32, (PART, BLK), 0) + layer * PART
    centre = (row >= BLK) & (row < 2 * BLK)
    for q in range(3):
        lanes = slice(q * BLK, (q + 1) * BLK)
        ends = jnp.where(first, keep[0:1, q : q + 1], keep[2:3, q : q + 1]).astype(F32)
        scale = jnp.where(centre, keep[1:2, q : q + 1].astype(F32), ends)
        out[:, lanes] = value[:, lanes] * scale


def shift(value, axis, steps):
    count = lax.axis_size(axis)
    return lax.ppermute(value, axis, [(i, (i + steps) % count) for i in range(count)])


def after(value, *earlier):
    return lax.optimization_barrier((value, *earlier))[0]


def shards(left_values, left_mask, right_values, right_mask, keep_mask):
    count = lax.axis_size("row")
    cols = lax.axis_size("col")
    z, col, layer = lax.axis_index("row"), lax.axis_index("col"), lax.axis_index("layer")
    place = jnp.stack([z, col, layer]).astype(jnp.int32)
    packed = jax.ShapeDtypeStruct((TILE + PART, BLK), F32)
    half = jax.ShapeDtypeStruct((PART, TILE), F32)
    whole = jax.ShapeDtypeStruct((TILE, TILE), F32)
    mask = pltpu.VMEM((3, 3), jnp.int32)

    left, right = call(
        prep_kernel, (packed, half), [SMEM] + [ANY] * 4,
        [mask, mask, pltpu.VMEM((TILE, TILE), F32), pltpu.VMEM((TILE, TILE), F32), pltpu.SemaphoreType.DMA((4,))],
        nbytes=2**21, limit=60,
    )(place, left_mask, right_mask, left_values, right_values)

    with jax.named_scope("left_x"):
        left_x = lax.ppermute(left, "col", [(i, i ^ 2) for i in range(cols)])
    pair = jnp.stack([left, left_x])
    pieces = [pair]

    reach = count // 2
    early, late = tuple(range(reach - 2)), (reach - 2, reach - 1)
    rights, behind, ahead = [right], right, right
    for step in range(1, reach):
        if 4 <= step <= 6:
            behind, ahead = after(behind, pieces[step - 3]), after(ahead, pieces[step - 3])
        with jax.named_scope(f"behind{step}"):
            behind = shift(behind, "row", 1)
        with jax.named_scope(f"ahead{step}"):
            ahead = shift(ahead, "row", -1)
        rights += [behind, ahead]
        if step <= 3:
            with jax.named_scope(f"left_y{step}"):
                pair = after(pair, behind, ahead)
                pieces.append(lax.ppermute(pair, "col", [(i, (i + 4 * step) % cols) for i in range(cols)]))
        if step == reach - 3:
            with jax.named_scope("left_core"):
                same = after(jnp.stack(pieces), behind, ahead)
                other = lax.ppermute(same, "col", [(i, i ^ 1) for i in range(cols)])

    n = 2 * len(early) - 1
    part = jax.ShapeDtypeStruct((TILE, len(late) * TILE), BF16)
    lefts, downs = pltpu.VMEM((TILE, len(early) * TILE), BF16), pltpu.VMEM((len(early) * TILE, TILE), BF16)
    total, far, late_h, late_l = call(
        functools.partial(main_kernel, early, late), (whole, packed, part, part), [SMEM] + [VMEM] * (2 + n),
        [lefts, lefts, downs, downs],
        flops=6 * TILE**3 * len(early), nbytes=10 * 2**20,
    )(place, same, other, *rights[:n])
    downs = pltpu.VMEM((len(late) * TILE, TILE), BF16)
    own, away = call(
        near_kernel, (half, half), [SMEM] + [VMEM] * (3 + 2 * len(late)), [downs, downs],
        flops=6 * TILE**3 * len(late), nbytes=2**21,
    )(place, total, late_h, late_l, *rights[n:])
    with jax.named_scope("away"):
        came = shift(away, "layer", 1)
    behind, ahead = after(behind, away), after(ahead, away)
    with jax.named_scope("behind8"):
        far_own = shift(behind, "row", 1)
    cross = [(z0 * 2 + l0, (z0 - 1) % count * 2 + 1 - l0) for z0 in range(count) for l0 in range(2)]
    with jax.named_scope("ahead8"):
        far_other = lax.ppermute(ahead, ("row", "layer"), cross)
    return call(last_kernel, half, [SMEM] + [VMEM] * 6, flops=6 * PART * TILE * TILE, nbytes=2**20)(
        place, keep_mask, own, came, far, far_own, far_other
    )


def solution(mesh):
    specs = (P("row", "col"),) * 5
    return jax.shard_map(shards, mesh=mesh, in_specs=specs, out_specs=P(("row", "layer"), "col"), check_vma=False)
```

```python
import functools
import itertools

import jax
import jax.numpy as jnp
from jax import lax
from jax.experimental import pallas as pl
from jax.experimental.pallas import tpu as pltpu
from jax.sharding import PartitionSpec as P

BLK = 128
HALF = 64
TILE = 3 * BLK
PART = TILE // 2
F32 = jnp.float32
BF16 = jnp.bfloat16
VMEM = pl.BlockSpec(memory_space=pltpu.VMEM)
SMEM = pl.BlockSpec(memory_space=pltpu.SMEM)
ANY = pl.BlockSpec(memory_space=pl.ANY)


def call(kernel, out_shapes, in_specs, scratch=(), flops=0, nbytes=0, limit=20):
    return pl.pallas_call(
        kernel,
        out_shape=out_shapes,
        in_specs=in_specs,
        out_specs=jax.tree.map(lambda _: VMEM, out_shapes),
        scratch_shapes=scratch,
        compiler_params=pltpu.CompilerParams(vmem_limit_bytes=limit * 2**20),
        cost_estimate=pl.CostEstimate(flops=flops, bytes_accessed=nbytes, transcendentals=0),
    )


def swap_halves(value):
    return pltpu.roll(value, HALF, 1)


def low_lanes(shape):
    return lax.broadcasted_iota(jnp.int32, shape, 1) < HALF


def fetch(pairs, sems):
    copies = [pltpu.make_async_copy(src, dst, sems.at[i]) for i, (src, dst) in enumerate(pairs)]
    for copy in copies:
        copy.start()
    return copies


def masked(values, mask, p, q, rows=slice(0, BLK)):
    block = values[p * BLK + rows.start : p * BLK + rows.stop, q * BLK : (q + 1) * BLK]
    return block * mask[p : p + 1, q : q + 1].astype(F32)


def prep_kernel(place, lm_in, rm_in, left_in, right_in, left_out, right_out, lm, rm, left, right, sems):
    z, col, layer = place[0], place[1], place[2]
    for copy in fetch(((rm_in, rm), (right_in, right), (lm_in, lm), (left_in, left)), sems):
        copy.wait()
    far = lax.rem(z + 8, 16) == col

    def right_side(outer, near):
        rows = slice(near * HALF, (near + 1) * HALF)
        for q in range(3):
            lanes = slice(q * BLK, (q + 1) * BLK)
            right_out[:BLK, lanes] = masked(right, rm, outer, q)
            right_out[BLK:, lanes] = masked(right, rm, 1, q, rows)

    def left_side(outer, near):
        for p in range(3):
            left_out[p * BLK : (p + 1) * BLK, :] = masked(left, lm, p, outer)
        middle = jnp.concatenate([masked(left, lm, p, 1) for p in range(3)], 0)
        top, bottom = middle[:PART], middle[PART:]
        keep_low = low_lanes((PART, BLK))
        if near == 0:
            left_out[TILE:, :] = jnp.where(keep_low, top, swap_halves(bottom))
        else:
            left_out[TILE:, :] = jnp.where(keep_low, swap_halves(top), bottom)

    def left_far(outer, near):
        for q in range(3):
            start = q * PART
            end = masked(left, lm, outer, q)
            mid = masked(left, lm, 1, q, slice(near * HALF, (near + 1) * HALF))
            left_out[start : start + PART, :] = jnp.concatenate([end, mid] if near == 0 else [mid, end], 0)

    for side in (0, 1):

        @pl.when(layer == side)
        def _(outer=2 * side, near=side):
            right_side(outer, near)
            pl.when(far)(lambda: left_far(outer, near))
            pl.when(jnp.logical_not(far))(lambda: left_side(outer, near))


def split(value):
    high = value.astype(BF16)
    return high, (value - high.astype(F32)).astype(BF16)


def triple(left, right):
    (lh, ll), (rh, rl) = left, right
    dot = functools.partial(jnp.dot, preferred_element_type=F32)
    return dot(lh, rh) + (dot(lh, rl) + dot(ll, rh))


def join_left(one, two):
    m1, m2 = one[TILE:], two[TILE:]
    keep_low = low_lanes((PART, BLK))
    top = jnp.where(keep_low, m1, swap_halves(m2))
    bottom = jnp.where(keep_low, swap_halves(m1), m2)
    return jnp.concatenate([one[:TILE], two[:TILE], jnp.concatenate([top, bottom], 0)], 1)


def join_right(one, two):
    return jnp.concatenate([one[:BLK], two[:BLK], one[BLK:], two[BLK:]], 0)


def panel_index(place, k):
    col = place[1]
    mine = lax.rem(k, 2) == lax.rem(col, 2)
    return mine, lax.rem(col // 4 - k // 4 + 4, 4), lax.bitwise_xor(lax.rem(k // 2, 2), lax.rem(col // 2, 2))


def tile_at(place, step):
    z, core = place[0], lax.rem(place[1], 2)
    return lax.rem(z + (2 * core - 1) * step + 16, 16)


def fill_left(place, same, other, one, two, lh, ll, column):
    mine1, y1, x1 = panel_index(place, one)
    mine2, y2, x2 = panel_index(place, one if two is None else two)
    span = slice(column, column + TILE)

    def put(panel1, panel2):
        first = panel1[y1, x1]
        second = jnp.zeros_like(first) if two is None else panel2[y2, x2]
        lh[:, span], ll[:, span] = split(join_left(first, second))

    for is1 in (True, False):
        for is2 in (True, False):
            pl.when((mine1 == is1) & (mine2 == is2))(
                functools.partial(put, same if is1 else other, same if is2 else other)
            )


def fill_right(one, two, rh, rl, row, lane=0):
    rows, lanes = slice(row, row + TILE), slice(lane, lane + TILE)
    rh[rows, lanes], rl[rows, lanes] = split(join_right(one, two))


def main_kernel(steps, place, same, other, *refs):
    mine, others = refs[:steps], refs[steps : 2 * steps]
    total, spare, far, late_h, late_l, lh, ll, rh, rl = refs[2 * steps :]
    core = lax.rem(place[1], 2)
    for start in range(0, steps, 2):
        column = start * PART
        paired = start + 1 < steps
        one, two = tile_at(place, start), tile_at(place, start + 1) if paired else None
        fill_left(place, same, other, one, two, lh, ll, column)
        for lane, tiles in ((0, mine), (TILE, others)):
            one = tiles[start][...]
            if start == 0:
                one = jnp.where(core == 0, one, jnp.zeros_like(one))
            two = tiles[start + 1][...] if paired else jnp.zeros_like(one)
            fill_right(one, two, rh, rl, column, lane)
    value = triple((lh[...], ll[...]), (rh[...], rl[...]))
    total[...] = value[:, :TILE]
    spare[...] = value[:, TILE:]
    fill_left(place, same, other, tile_at(place, steps), tile_at(place, -steps), late_h, late_l, 0)
    here, y, x = panel_index(place, lax.rem(place[0] + 8, 16))

    @pl.when(here)
    def _():
        far[...] = same[y, x]

    @pl.when(jnp.logical_not(here))
    def _():
        far[...] = other[y, x]


def near_kernel(place, total, spare, late_h, late_l, one, two, own, away, rh, rl):
    fill_right(one[...], two[...], rh, rl, 0)
    value = total[...] + spare[...] + triple((late_h[...], late_l[...]), (rh[...], rl[...]))
    layer = place[2]

    @pl.when(layer == 0)
    def _():
        own[...] = value[:PART]
        away[...] = value[PART:]

    @pl.when(layer == 1)
    def _():
        own[...] = value[PART:]
        away[...] = value[:PART]


def last_kernel(place, keep, own, came, far, right_own, right_other, out):
    layer = place[2]
    first = layer == 0
    mine, other = right_own[...], right_other[...]
    low, high = jnp.where(first, mine, other), jnp.where(first, other, mine)
    right = jnp.concatenate([low, high[BLK:], high[:BLK]], 0)
    left = jnp.concatenate([far[:PART], far[PART : 2 * PART], far[2 * PART :]], 1)
    value = own[...] + came[...] + triple(split(left), split(right))
    row = lax.broadcasted_iota(jnp.int32, (PART, BLK), 0) + layer * PART
    centre = (row >= BLK) & (row < 2 * BLK)
    for q in range(3):
        lanes = slice(q * BLK, (q + 1) * BLK)
        ends = jnp.where(first, keep[0:1, q : q + 1], keep[2:3, q : q + 1]).astype(F32)
        scale = jnp.where(centre, keep[1:2, q : q + 1].astype(F32), ends)
        out[:, lanes] = value[:, lanes] * scale


def move(value, axes, target):
    sizes = [lax.axis_size(axis) for axis in axes]
    flat = lambda at: functools.reduce(lambda total, pair: total * pair[1] + pair[0] % pair[1], zip(at, sizes), 0)
    points = list(itertools.product(*map(range, sizes)))
    return lax.ppermute(value, axes, [(flat(at), flat(target(*at))) for at in points])


def along(core):
    return 1 - 2 * core


def onward(value):
    return move(value, ("row", "col"), lambda z, c: (z + along(c % 2), c))


def after(value, *earlier):
    return lax.optimization_barrier((value, *earlier))[0]


def shards(left_values, left_mask, right_values, right_mask, keep_mask):
    count = lax.axis_size("row")
    cols = lax.axis_size("col")
    z, col, layer = lax.axis_index("row"), lax.axis_index("col"), lax.axis_index("layer")
    place = jnp.stack([z, col, layer]).astype(jnp.int32)
    packed = jax.ShapeDtypeStruct((TILE + PART, BLK), F32)
    half = jax.ShapeDtypeStruct((PART, TILE), F32)
    whole = jax.ShapeDtypeStruct((TILE, TILE), F32)
    mask = pltpu.VMEM((3, 3), jnp.int32)

    left, right = call(
        prep_kernel, (packed, half), [SMEM] + [ANY] * 4,
        [mask, mask, pltpu.VMEM((TILE, TILE), F32), pltpu.VMEM((TILE, TILE), F32), pltpu.SemaphoreType.DMA((4,))],
        nbytes=2**21, limit=60,
    )(place, left_mask, right_mask, left_values, right_values)

    with jax.named_scope("right_core"):
        right_other = move(right, ("col",), lambda c: (c ^ 1,))
    with jax.named_scope("left_x"):
        left_x = move(left, ("col",), lambda c: (c ^ 2,))
    pair = jnp.stack([left, left_x])
    pieces = [pair]

    steps = count // 2 - 1
    mine, others = [right], [right_other]
    one, two = right, right_other
    for step in range(1, steps + 1):
        if 4 <= step <= 6:
            one, two = after(one, pieces[step - 3]), after(two, pieces[step - 3])
        with jax.named_scope(f"own{step}"):
            one = onward(one)
        with jax.named_scope(f"other{step}"):
            if step < steps:
                two = onward(two)
            else:
                two = move(two, ("row", "col"), lambda z, c: (z + along(c % 2), c ^ 1))
        mine.append(one)
        others.append(two)
        if step <= 3:
            with jax.named_scope(f"left_y{step}"):
                pair = after(pair, one, two)
                pieces.append(move(pair, ("col",), lambda c: (c + 4 * step,)))
        if step == steps - 2:
            with jax.named_scope("left_core"):
                same = after(jnp.stack(pieces), one, two)
                other = move(same, ("col",), lambda c: (c ^ 1,))

    span = (steps + 1) // 2 * TILE
    part = jax.ShapeDtypeStruct((TILE, TILE), BF16)
    lefts, rights = pltpu.VMEM((TILE, span), BF16), pltpu.VMEM((span, 2 * TILE), BF16)
    total, spare, far, late_h, late_l = call(
        functools.partial(main_kernel, steps), (whole, whole, packed, part, part), [SMEM] + [VMEM] * (2 + 2 * steps),
        [lefts, lefts, rights, rights], flops=12 * span * TILE**2, nbytes=10 * 2**20,
    )(place, same, other, *mine[:steps], *others[:steps])
    with jax.named_scope("spare"):
        spare = move(spare, ("col",), lambda c: (c ^ 1,))
    rights = pltpu.VMEM((TILE, TILE), BF16)
    own, away = call(
        near_kernel, (half, half), [SMEM] + [VMEM] * 6, [rights, rights], flops=6 * TILE**3, nbytes=2**21
    )(place, total, spare, late_h, late_l, one, two)
    with jax.named_scope("away"):
        came = move(away, ("layer",), lambda l: (1 - l,))
    one, two = after(one, away), after(two, away)
    with jax.named_scope("far_own"):
        far_own = onward(one)
    with jax.named_scope("far_other"):
        far_other = move(two, ("row", "col", "layer"), lambda z, c, l: (z - along(c % 2), c, 1 - l))
    return call(last_kernel, half, [SMEM] + [VMEM] * 6, flops=6 * PART * TILE * TILE, nbytes=2**20)(
        place, keep_mask, own, came, far, far_own, far_other
    )


def solution(mesh):
    specs = (P("row", "col"),) * 5
    return jax.shard_map(shards, mesh=mesh, in_specs=specs, out_specs=P(("row", "layer"), "col"), check_vma=False)
```

```python
import functools
import itertools

import jax
import jax.numpy as jnp
from jax import lax
from jax.experimental import pallas as pl
from jax.experimental.pallas import tpu as pltpu
from jax.sharding import PartitionSpec as P

BLK = 128
HALF = 64
TILE = 3 * BLK
PART = TILE // 2
F32 = jnp.float32
BF16 = jnp.bfloat16
VMEM = pl.BlockSpec(memory_space=pltpu.VMEM)
ANY = pl.BlockSpec(memory_space=pl.ANY)


def call(kernel, out_shapes, in_specs, scratch=(), flops=0, nbytes=0, limit=20):
    return pl.pallas_call(
        kernel,
        out_shape=out_shapes,
        in_specs=in_specs,
        out_specs=jax.tree.map(lambda _: VMEM, out_shapes),
        scratch_shapes=scratch,
        compiler_params=pltpu.CompilerParams(vmem_limit_bytes=limit * 2**20),
        cost_estimate=pl.CostEstimate(flops=flops, bytes_accessed=nbytes, transcendentals=0),
    )


def swap_halves(value):
    return pltpu.roll(value, HALF, 1)


def low_lanes(shape):
    return lax.broadcasted_iota(jnp.int32, shape, 1) < HALF


def fetch(pairs, sems):
    copies = [pltpu.make_async_copy(src, dst, sems.at[i]) for i, (src, dst) in enumerate(pairs)]
    for copy in copies:
        copy.start()
    return copies


def masked(values, mask, p, q, rows=slice(0, BLK)):
    block = values[p * BLK + rows.start : p * BLK + rows.stop, q * BLK : (q + 1) * BLK]
    return block * mask[p : p + 1, q : q + 1].astype(F32)


def coordinates():
    return lax.axis_index("row"), lax.axis_index("col"), lax.axis_index("layer")


def prep_kernel(lm_in, rm_in, left_in, right_in, left_out, right_out, lm, rm, left, right, sems):
    place = coordinates()
    z, col, layer = place[0], place[1], place[2]
    copies = fetch(((rm_in, rm), (right_in, right), (lm_in, lm), (left_in, left)), sems)
    far = lax.rem(z + 8, 16) == col

    def right_side(outer, near):
        rows = slice(near * HALF, (near + 1) * HALF)
        for q in range(3):
            lanes = slice(q * BLK, (q + 1) * BLK)
            right_out[:BLK, lanes] = masked(right, rm, outer, q)
            right_out[BLK:, lanes] = masked(right, rm, 1, q, rows)

    def left_side(outer, near):
        for p in range(3):
            left_out[p * BLK : (p + 1) * BLK, :] = masked(left, lm, p, outer)
        middle = jnp.concatenate([masked(left, lm, p, 1) for p in range(3)], 0)
        top, bottom = middle[:PART], middle[PART:]
        keep_low = low_lanes((PART, BLK))
        if near == 0:
            left_out[TILE:, :] = jnp.where(keep_low, top, swap_halves(bottom))
        else:
            left_out[TILE:, :] = jnp.where(keep_low, swap_halves(top), bottom)

    def left_far(outer, near):
        for q in range(3):
            start = q * PART
            end = masked(left, lm, outer, q)
            mid = masked(left, lm, 1, q, slice(near * HALF, (near + 1) * HALF))
            left_out[start : start + PART, :] = jnp.concatenate([end, mid] if near == 0 else [mid, end], 0)

    copies[0].wait()
    copies[1].wait()
    for side in (0, 1):
        pl.when(layer == side)(functools.partial(right_side, 2 * side, side))
    copies[2].wait()
    copies[3].wait()
    for side in (0, 1):
        pl.when((layer == side) & far)(functools.partial(left_far, 2 * side, side))
        pl.when((layer == side) & jnp.logical_not(far))(functools.partial(left_side, 2 * side, side))


def split(value):
    high = value.astype(BF16)
    return high, (value - high.astype(F32)).astype(BF16)


def triple(left, right):
    (lh, ll), (rh, rl) = left, right
    dot = functools.partial(jnp.dot, preferred_element_type=F32)
    return dot(lh, rh) + (dot(lh, rl) + dot(ll, rh))


def join_left(one, two):
    m1, m2 = one[TILE:], two[TILE:]
    keep_low = low_lanes((PART, BLK))
    top = jnp.where(keep_low, m1, swap_halves(m2))
    bottom = jnp.where(keep_low, swap_halves(m1), m2)
    return jnp.concatenate([one[:TILE], two[:TILE], jnp.concatenate([top, bottom], 0)], 1)


def join_right(one, two):
    return jnp.concatenate([one[:BLK], two[:BLK], one[BLK:], two[BLK:]], 0)


def along(core):
    return 1 - 2 * core


def panel_index(place, k):
    col, core = place[1], lax.rem(k, 2)
    hops = lax.rem((col // 4 - k // 4) * along(core) + 4, 4)
    return core == lax.rem(col, 2), hops, lax.bitwise_xor(lax.rem(k // 2, 2), lax.rem(col // 2, 2))


def tile_at(place, step):
    z, core = place[0], lax.rem(place[1], 2)
    return lax.rem(z + (2 * core - 1) * step + 16, 16)


def fill_left(place, same, other, one, two, lh, ll, column):
    mine1, y1, x1 = panel_index(place, one)
    mine2, y2, x2 = panel_index(place, one if two is None else two)
    span = slice(column, column + TILE)

    def put(panel1, panel2):
        first = panel1[y1, x1]
        second = jnp.zeros_like(first) if two is None else panel2[y2, x2]
        lh[:, span], ll[:, span] = split(join_left(first, second))

    for is1 in (True, False):
        for is2 in (True, False):
            pl.when((mine1 == is1) & (mine2 == is2))(
                functools.partial(put, same if is1 else other, same if is2 else other)
            )


def fill_right(one, two, rh, rl, row, lane=0):
    rows, lanes = slice(row, row + TILE), slice(lane, lane + TILE)
    rh[rows, lanes], rl[rows, lanes] = split(join_right(one, two))


def fill_rights(place, tiles, rh, rl):
    core = lax.rem(place[1], 2)
    for start in range(0, len(tiles), 2):
        one = tiles[start][...]
        if start == 0:
            one = jnp.where(core == 0, one, jnp.zeros_like(one))
        two = tiles[start + 1][...] if start + 1 < len(tiles) else jnp.zeros_like(one)
        fill_right(one, two, rh, rl, start * PART)


def spare_kernel(steps, same, other, *refs):
    place = coordinates()
    tiles, (spare, lh, ll, far, late_h, late_l, rh, rl) = refs[:steps], refs[steps:]
    for start in range(0, steps, 2):
        two = tile_at(place, start + 1) if start + 1 < steps else None
        fill_left(place, same, other, tile_at(place, start), two, lh, ll, start * PART)
    fill_rights(place, tiles, rh, rl)
    spare[...] = triple((lh[...], ll[...]), (rh[...], rl[...]))
    for number, step in enumerate((steps, steps + 1)):
        fill_left(place, same, other, tile_at(place, step), tile_at(place, -step), late_h, late_l, number * TILE)
    here, y, x = panel_index(place, lax.rem(place[0] + 8, 16))

    @pl.when(here)
    def _():
        far[...] = same[y, x]

    @pl.when(jnp.logical_not(here))
    def _():
        far[...] = other[y, x]


def main_kernel(steps, lh, ll, *refs):
    place = coordinates()
    tiles, (total, rh, rl) = refs[:steps], refs[steps:]
    fill_rights(place, tiles, rh, rl)
    total[...] = triple((lh[...], ll[...]), (rh[...], rl[...]))


def near_kernel(total, spare, late_h, late_l, one, two, three, four, own, away, rh, rl):
    place = coordinates()
    fill_right(one[...], two[...], rh, rl, 0)
    fill_right(three[...], four[...], rh, rl, TILE)
    value = total[...] + spare[...] + triple((late_h[...], late_l[...]), (rh[...], rl[...]))
    layer = place[2]
    away[PART:] = jnp.zeros((8, TILE), F32)

    @pl.when(layer == 0)
    def _():
        own[...] = value[:PART]
        away[:PART] = value[PART:]

    @pl.when(layer == 1)
    def _():
        own[...] = value[PART:]
        away[:PART] = value[:PART]


def last_kernel(keep, own, came, far, right_own, right_other, out):
    place = coordinates()
    layer = place[2]
    first = layer == 0
    mine, other = right_own[...], right_other[...]
    low, high = jnp.where(first, mine, other), jnp.where(first, other, mine)
    right = jnp.concatenate([low, high[BLK:], high[:BLK]], 0)
    left = jnp.concatenate([far[:PART], far[PART : 2 * PART], far[2 * PART :]], 1)
    value = own[...] + came[:PART] + triple(split(left), split(right))
    row = lax.broadcasted_iota(jnp.int32, (PART, BLK), 0) + layer * PART
    centre = (row >= BLK) & (row < 2 * BLK)
    for q in range(3):
        lanes = slice(q * BLK, (q + 1) * BLK)
        ends = jnp.where(first, keep[0:1, q : q + 1], keep[2:3, q : q + 1]).astype(F32)
        scale = jnp.where(centre, keep[1:2, q : q + 1].astype(F32), ends)
        out[:, lanes] = value[:, lanes] * scale


def move(value, axes, target):
    sizes = [lax.axis_size(axis) for axis in axes]
    flat = lambda at: functools.reduce(lambda total, pair: total * pair[1] + pair[0] % pair[1], zip(at, sizes), 0)
    points = list(itertools.product(*map(range, sizes)))
    return lax.ppermute(value, axes, [(flat(at), flat(target(*at))) for at in points])


def onward(value):
    return move(value, ("row", "col"), lambda z, c: (z + along(c % 2), c))


def after(value, *earlier):
    return lax.optimization_barrier((value, *earlier))[0]


def shards(left_values, left_mask, right_values, right_mask, keep_mask):
    count = lax.axis_size("row")
    packed = jax.ShapeDtypeStruct((TILE + PART, BLK), F32)
    half = jax.ShapeDtypeStruct((PART, TILE), F32)
    whole = jax.ShapeDtypeStruct((TILE, TILE), F32)
    mask = pltpu.VMEM((3, 3), jnp.int32)

    left, right = call(
        prep_kernel, (packed, half), [ANY] * 4,
        [mask, mask, pltpu.VMEM((TILE, TILE), F32), pltpu.VMEM((TILE, TILE), F32), pltpu.SemaphoreType.DMA((4,))],
        nbytes=2**21, limit=60,
    )(left_mask, right_mask, left_values, right_values)

    with jax.named_scope("right_core"):
        right_other = move(right, ("col",), lambda c: (c ^ 1,))
    with jax.named_scope("left_x"):
        left_x = move(left, ("col",), lambda c: (c ^ 2,))
    pair = jnp.stack([left, left_x])

    steps = count // 2 - 1
    mine, others = [right], [right_other]
    one, two = right, right_other
    for step in range(1, steps + 1):
        if step == 3:
            one, two = after(one, pair), after(two, pair)
        with jax.named_scope(f"own{step}"):
            one = onward(one)
        with jax.named_scope(f"other{step}"):
            if step < steps:
                two = onward(two)
            else:
                two = move(two, ("row", "col"), lambda z, c: (z + along(c % 2), c ^ 1))
        mine.append(one)
        others.append(two)
        if step == 1:
            with jax.named_scope("left_y1"):
                left_y1 = move(after(pair, one, two), ("col",), lambda c: (c + 4 * along(c % 2),))
        if step == 2:
            with jax.named_scope("left_y3"):
                left_y3 = move(after(pair, one, two), ("col",), lambda c: (c - 4 * along(c % 2),))
        if step == 3:
            with jax.named_scope("left_y2"):
                left_y2 = move(after(left_y1, one), ("col",), lambda c: (c + 4 * along(c % 2),))
        if step == 5:
            with jax.named_scope("left_core"):
                same = after(jnp.stack([pair, left_y1, left_y2, left_y3]), one, two)
                other = move(same, ("col",), lambda c: (c ^ 1,))

    with jax.named_scope("crossed"):
        crossed = move(others[steps - 1], ("col",), lambda c: (c ^ 1,))
    early = steps - 1
    span = early * PART
    part = jax.ShapeDtypeStruct((TILE, 2 * TILE), BF16)
    lefts = jax.ShapeDtypeStruct((TILE, span), BF16)
    rights = [pltpu.VMEM((span, TILE), BF16)] * 2
    spare, left_h, left_l, far, late_h, late_l = call(
        functools.partial(spare_kernel, early), (whole, lefts, lefts, packed, part, part), [VMEM] * (2 + early),
        rights, flops=6 * span * TILE**2, nbytes=6 * 2**20,
    )(same, other, *others[:early])
    total = call(
        functools.partial(main_kernel, early), whole, [VMEM] * (2 + early), rights,
        flops=6 * span * TILE**2, nbytes=4 * 2**20,
    )(left_h, left_l, *mine[:early])
    with jax.named_scope("spare"):
        spare = move(spare, ("col",), lambda c: (c ^ 1,))
    rights = pltpu.VMEM((2 * TILE, TILE), BF16)
    own, away = call(
        near_kernel, (half, jax.ShapeDtypeStruct((PART + 8, TILE), F32)), [VMEM] * 8, [rights, rights], flops=12 * TILE**3, nbytes=2**21
    )(total, spare, late_h, late_l, mine[early], crossed, one, two)
    with jax.named_scope("away"):
        came = move(away, ("layer",), lambda l: (1 - l,))
    one, two = after(one, away), after(two, away)
    with jax.named_scope("far_own"):
        far_own = onward(one)
    with jax.named_scope("far_other"):
        far_other = move(two, ("row", "col", "layer"), lambda z, c, l: (z - along(c % 2), c, 1 - l))
    return call(last_kernel, half, [VMEM] * 6, flops=6 * PART * TILE * TILE, nbytes=2**20)(
        keep_mask, own, came, far, far_own, far_other
    )


def solution(mesh):
    specs = (P("row", "col"),) * 5
    return jax.shard_map(shards, mesh=mesh, in_specs=specs, out_specs=P(("row", "layer"), "col"), check_vma=False)
```

```python
import functools
import itertools

import jax
import jax.numpy as jnp
from jax import lax
from jax.experimental import pallas as pl
from jax.experimental.pallas import tpu as pltpu
from jax.sharding import PartitionSpec as P

BLK = 128
HALF = 64
TILE = 3 * BLK
PART = TILE // 2
F32 = jnp.float32
BF16 = jnp.bfloat16
VMEM = pl.BlockSpec(memory_space=pltpu.VMEM)
ANY = pl.BlockSpec(memory_space=pl.ANY)


def call(kernel, out_shapes, in_specs, scratch=(), flops=0, nbytes=0, limit=20):
    return pl.pallas_call(
        kernel,
        out_shape=out_shapes,
        in_specs=in_specs,
        out_specs=jax.tree.map(lambda _: VMEM, out_shapes),
        scratch_shapes=scratch,
        compiler_params=pltpu.CompilerParams(vmem_limit_bytes=limit * 2**20),
        cost_estimate=pl.CostEstimate(flops=flops, bytes_accessed=nbytes, transcendentals=0),
    )


def swap_halves(value):
    return pltpu.roll(value, HALF, 1)


def low_lanes(shape):
    return lax.broadcasted_iota(jnp.int32, shape, 1) < HALF


def fetch(pairs, sems):
    copies = [pltpu.make_async_copy(src, dst, sems.at[i]) for i, (src, dst) in enumerate(pairs)]
    for copy in copies:
        copy.start()
    return copies


def masked(values, mask, p, q, rows=slice(0, BLK)):
    block = values[p * BLK + rows.start : p * BLK + rows.stop, q * BLK : (q + 1) * BLK]
    return block * mask[p : p + 1, q : q + 1].astype(F32)


def coordinates():
    return lax.axis_index("row"), lax.axis_index("col"), lax.axis_index("layer")


def prep_kernel(lm_in, rm_in, left_in, right_in, left_out, right_out, lm, rm, left, right, sems):
    place = coordinates()
    z, col, layer = place[0], place[1], place[2]
    copies = fetch(((rm_in, rm), (right_in, right), (lm_in, lm), (left_in, left)), sems)
    far = lax.rem(z + 8, 16) == col

    def right_side(outer, near):
        rows = slice(near * HALF, (near + 1) * HALF)
        for q in range(3):
            lanes = slice(q * BLK, (q + 1) * BLK)
            right_out[:BLK, lanes] = masked(right, rm, outer, q)
            right_out[BLK:, lanes] = masked(right, rm, 1, q, rows)

    def left_side(outer, near):
        for p in range(3):
            left_out[p * BLK : (p + 1) * BLK, :] = masked(left, lm, p, outer)
        middle = jnp.concatenate([masked(left, lm, p, 1) for p in range(3)], 0)
        top, bottom = middle[:PART], middle[PART:]
        keep_low = low_lanes((PART, BLK))
        if near == 0:
            left_out[TILE:, :] = jnp.where(keep_low, top, swap_halves(bottom))
        else:
            left_out[TILE:, :] = jnp.where(keep_low, swap_halves(top), bottom)

    def left_far(outer, near):
        for q in range(3):
            start = q * PART
            end = masked(left, lm, outer, q)
            mid = masked(left, lm, 1, q, slice(near * HALF, (near + 1) * HALF))
            left_out[start : start + PART, :] = jnp.concatenate([end, mid] if near == 0 else [mid, end], 0)

    copies[0].wait()
    copies[1].wait()
    for side in (0, 1):
        pl.when(layer == side)(functools.partial(right_side, 2 * side, side))
    copies[2].wait()
    copies[3].wait()
    for side in (0, 1):
        pl.when((layer == side) & far)(functools.partial(left_far, 2 * side, side))
        pl.when((layer == side) & jnp.logical_not(far))(functools.partial(left_side, 2 * side, side))


def split(value):
    high = value.astype(BF16)
    return high, (value - high.astype(F32)).astype(BF16)


def triple(left, right):
    (lh, ll), (rh, rl) = left, right
    dot = functools.partial(jnp.dot, preferred_element_type=F32)
    return dot(lh, rh) + (dot(lh, rl) + dot(ll, rh))


def join_left(one, two):
    m1, m2 = one[TILE:], two[TILE:]
    keep_low = low_lanes((PART, BLK))
    top = jnp.where(keep_low, m1, swap_halves(m2))
    bottom = jnp.where(keep_low, swap_halves(m1), m2)
    return jnp.concatenate([one[:TILE], two[:TILE], jnp.concatenate([top, bottom], 0)], 1)


def join_right(one, two):
    return jnp.concatenate([one[:BLK], two[:BLK], one[BLK:], two[BLK:]], 0)


def along(core):
    return 1 - 2 * core


def panel_index(place, k):
    col, core = place[1], lax.rem(k, 2)
    hops = lax.rem((col // 4 - k // 4) * along(core) + 4, 4)
    return core == lax.rem(col, 2), hops, lax.bitwise_xor(lax.rem(k // 2, 2), lax.rem(col // 2, 2))


def tile_at(place, step):
    z, core = place[0], lax.rem(place[1], 2)
    return lax.rem(z + (2 * core - 1) * step + 16, 16)


def fill_left(place, same, other, one, two, lh, ll, column):
    mine1, y1, x1 = panel_index(place, one)
    mine2, y2, x2 = panel_index(place, one if two is None else two)
    span = slice(column, column + TILE)

    def put(panel1, panel2):
        first = panel1[y1, x1]
        second = jnp.zeros_like(first) if two is None else panel2[y2, x2]
        lh[:, span], ll[:, span] = split(join_left(first, second))

    for is1 in (True, False):
        for is2 in (True, False):
            pl.when((mine1 == is1) & (mine2 == is2))(
                functools.partial(put, same if is1 else other, same if is2 else other)
            )


def fill_right(one, two, rh, rl, row, lane=0):
    rows, lanes = slice(row, row + TILE), slice(lane, lane + TILE)
    rh[rows, lanes], rl[rows, lanes] = split(join_right(one, two))


def fill_rights(tiles, rh, rl):
    held = [jnp.zeros((PART, TILE), F32) if tile is None else tile[...] for tile in tiles]
    for start in range(0, len(held), 2):
        fill_right(held[start], held[start + 1], rh, rl, start * PART)


def spare_kernel(steps, same, other, *refs):
    place = coordinates()
    tiles, (spare, lh, ll, far, late_h, late_l, rh, rl) = refs[: steps - 1], refs[steps - 1 :]
    for start in range(0, steps, 2):
        two = tile_at(place, start + 1) if start + 1 < steps else None
        fill_left(place, same, other, tile_at(place, start), two, lh, ll, start * PART)
    fill_rights((None, *tiles), rh, rl)
    spare[...] = triple((lh[...], ll[...]), (rh[...], rl[...]))
    for number, step in enumerate((steps, steps + 1)):
        fill_left(place, same, other, tile_at(place, step), tile_at(place, -step), late_h, late_l, number * TILE)
    here, y, x = panel_index(place, lax.rem(place[0] + 8, 16))

    @pl.when(here)
    def _():
        far[...] = same[y, x]

    @pl.when(jnp.logical_not(here))
    def _():
        far[...] = other[y, x]


def main_kernel(steps, lh, ll, *refs):
    tiles, (total, rh, rl) = refs[:steps], refs[steps:]
    fill_rights(tiles, rh, rl)
    total[...] = triple((lh[...], ll[...]), (rh[...], rl[...]))


def near_kernel(total, spare, late_h, late_l, one, two, three, four, own, away, rh, rl):
    place = coordinates()
    fill_right(one[...], two[...], rh, rl, 0)
    fill_right(three[...], four[...], rh, rl, TILE)
    value = total[...] + spare[...] + triple((late_h[...], late_l[...]), (rh[...], rl[...]))
    layer = place[2]
    away[PART:] = jnp.zeros((8, TILE), F32)

    @pl.when(layer == 0)
    def _():
        own[...] = value[:PART]
        away[:PART] = value[PART:]

    @pl.when(layer == 1)
    def _():
        own[...] = value[PART:]
        away[:PART] = value[:PART]


def last_kernel(keep, own, came, far, right_own, right_other, out):
    place = coordinates()
    layer = place[2]
    first = layer == 0
    mine, other = right_own[...], right_other[...]
    low, high = jnp.where(first, mine, other), jnp.where(first, other, mine)
    right = jnp.concatenate([low, high[BLK:], high[:BLK]], 0)
    left = jnp.concatenate([far[:PART], far[PART : 2 * PART], far[2 * PART :]], 1)
    value = own[...] + came[:PART] + triple(split(left), split(right))
    row = lax.broadcasted_iota(jnp.int32, (PART, BLK), 0) + layer * PART
    centre = (row >= BLK) & (row < 2 * BLK)
    for q in range(3):
        lanes = slice(q * BLK, (q + 1) * BLK)
        ends = jnp.where(first, keep[0:1, q : q + 1], keep[2:3, q : q + 1]).astype(F32)
        scale = jnp.where(centre, keep[1:2, q : q + 1].astype(F32), ends)
        out[:, lanes] = value[:, lanes] * scale


def move(value, axes, target):
    sizes = [lax.axis_size(axis) for axis in axes]
    flat = lambda at: functools.reduce(lambda total, pair: total * pair[1] + pair[0] % pair[1], zip(at, sizes), 0)
    points = list(itertools.product(*map(range, sizes)))
    return lax.ppermute(value, axes, [(flat(at), flat(target(*at))) for at in points])


def onward(value):
    return move(value, ("row", "col"), lambda z, c: (z + along(c % 2), c))


def after(value, *earlier):
    return lax.optimization_barrier((value, *earlier))[0]


def shards(left_values, left_mask, right_values, right_mask, keep_mask):
    count = lax.axis_size("row")
    packed = jax.ShapeDtypeStruct((TILE + PART, BLK), F32)
    half = jax.ShapeDtypeStruct((PART, TILE), F32)
    whole = jax.ShapeDtypeStruct((TILE, TILE), F32)
    mask = pltpu.VMEM((3, 3), jnp.int32)

    left, right = call(
        prep_kernel, (packed, half), [ANY] * 4,
        [mask, mask, pltpu.VMEM((TILE, TILE), F32), pltpu.VMEM((TILE, TILE), F32), pltpu.SemaphoreType.DMA((4,))],
        nbytes=2**21, limit=60,
    )(left_mask, right_mask, left_values, right_values)

    with jax.named_scope("left_x"):
        left_x = move(left, ("col",), lambda c: (c ^ 2,))
    pair = jnp.stack([left, left_x])

    steps = count // 2 - 1
    mine, others = [right], [None]
    one = two = right
    for step in range(1, steps + 1):
        if step == 3:
            one, two = after(one, pair), after(two, pair)
        with jax.named_scope(f"own{step}"):
            one = onward(one)
        with jax.named_scope(f"other{step}"):
            if step == 1:
                two = move(two, ("row", "col"), lambda z, c: (z - along(c % 2), c ^ 1))
            elif step < steps - 1:
                two = onward(two)
            elif step == steps - 1:
                two = move(two, ("row", "col"), lambda z, c: (z + along(c % 2), c ^ 1))
            else:
                two = move(two, ("row", "col"), lambda z, c: (z - along(c % 2), c))
        mine.append(one)
        others.append(two)
        if step == 1:
            with jax.named_scope("left_y1"):
                left_y1 = move(after(pair, one, two), ("col",), lambda c: (c + 4 * along(c % 2),))
        if step == 2:
            with jax.named_scope("left_y3"):
                left_y3 = move(after(pair, one, two), ("col",), lambda c: (c - 4 * along(c % 2),))
        if step == 3:
            with jax.named_scope("left_y2"):
                left_y2 = move(after(left_y1, one), ("col",), lambda c: (c + 4 * along(c % 2),))
        if step == 5:
            with jax.named_scope("left_core"):
                same = after(jnp.stack([pair, left_y1, left_y2, left_y3]), one, two)
                other = move(same, ("col",), lambda c: (c ^ 1,))

    early = steps - 1
    span = early * PART
    part = jax.ShapeDtypeStruct((TILE, 2 * TILE), BF16)
    lefts = jax.ShapeDtypeStruct((TILE, span), BF16)
    rights = [pltpu.VMEM((span, TILE), BF16)] * 2
    spare, left_h, left_l, far, late_h, late_l = call(
        functools.partial(spare_kernel, early), (whole, lefts, lefts, packed, part, part), [VMEM] * (1 + early),
        rights, flops=6 * span * TILE**2, nbytes=6 * 2**20,
    )(same, other, *others[1:early])
    total = call(
        functools.partial(main_kernel, early), whole, [VMEM] * (2 + early), rights,
        flops=6 * span * TILE**2, nbytes=4 * 2**20,
    )(left_h, left_l, *mine[:early])
    with jax.named_scope("spare"):
        spare = move(spare, ("col",), lambda c: (c ^ 1,))
    rights = pltpu.VMEM((2 * TILE, TILE), BF16)
    own, away = call(
        near_kernel, (half, jax.ShapeDtypeStruct((PART + 8, TILE), F32)), [VMEM] * 8, [rights, rights], flops=12 * TILE**3, nbytes=2**21
    )(total, spare, late_h, late_l, mine[early], others[early], one, two)
    with jax.named_scope("away"):
        came = move(away, ("layer",), lambda l: (1 - l,))
    one, two = after(one, away), after(two, away)
    with jax.named_scope("far_own"):
        far_own = onward(one)
    with jax.named_scope("far_other"):
        far_other = move(two, ("row", "col", "layer"), lambda z, c, l: (z - along(c % 2), c, 1 - l))
    return call(last_kernel, half, [VMEM] * 6, flops=6 * PART * TILE * TILE, nbytes=2**20)(
        keep_mask, own, came, far, far_own, far_other
    )


def solution(mesh):
    specs = (P("row", "col"),) * 5
    return jax.shard_map(shards, mesh=mesh, in_specs=specs, out_specs=P(("row", "layer"), "col"), check_vma=False)
```

```python
import functools
import itertools

import jax
import jax.numpy as jnp
from jax import lax
from jax.experimental import pallas as pl
from jax.experimental.pallas import tpu as pltpu
from jax.sharding import PartitionSpec as P

BLK = 128
HALF = 64
TILE = 3 * BLK
PART = TILE // 2
F32 = jnp.float32
BF16 = jnp.bfloat16
VMEM = pl.BlockSpec(memory_space=pltpu.VMEM)
ANY = pl.BlockSpec(memory_space=pl.ANY)


def call(kernel, out_shapes, in_specs, scratch=(), flops=0, nbytes=0, limit=20):
    return pl.pallas_call(
        kernel,
        out_shape=out_shapes,
        in_specs=in_specs,
        out_specs=jax.tree.map(lambda _: VMEM, out_shapes),
        scratch_shapes=scratch,
        compiler_params=pltpu.CompilerParams(vmem_limit_bytes=limit * 2**20),
        cost_estimate=pl.CostEstimate(flops=flops, bytes_accessed=nbytes, transcendentals=0),
    )


def swap_halves(value):
    return pltpu.roll(value, HALF, 1)


def low_lanes(shape):
    return lax.broadcasted_iota(jnp.int32, shape, 1) < HALF


def fetch(pairs, sems):
    copies = [pltpu.make_async_copy(src, dst, sems.at[i]) for i, (src, dst) in enumerate(pairs)]
    for copy in copies:
        copy.start()
    return copies


def masked(values, mask, p, q, rows=slice(0, BLK)):
    block = values[p * BLK + rows.start : p * BLK + rows.stop, q * BLK : (q + 1) * BLK]
    return block * mask[p : p + 1, q : q + 1].astype(F32)


def coordinates():
    return lax.axis_index("row"), lax.axis_index("col"), lax.axis_index("layer")


def prep_kernel(lm_in, rm_in, left_in, right_in, left_out, right_out, lm, rm, left, right, sems):
    place = coordinates()
    z, col, layer = place[0], place[1], place[2]
    copies = fetch(((rm_in, rm), (right_in, right), (lm_in, lm), (left_in, left)), sems)
    far = lax.rem(z + 8, 16) == col

    def right_side(outer, near):
        rows = slice(near * HALF, (near + 1) * HALF)
        for q in range(3):
            lanes = slice(q * BLK, (q + 1) * BLK)
            right_out[:BLK, lanes] = masked(right, rm, outer, q)
            right_out[BLK:, lanes] = masked(right, rm, 1, q, rows)

    def left_side(outer, near):
        for p in range(3):
            left_out[p * BLK : (p + 1) * BLK, :] = masked(left, lm, p, outer)
        middle = jnp.concatenate([masked(left, lm, p, 1) for p in range(3)], 0)
        top, bottom = middle[:PART], middle[PART:]
        keep_low = low_lanes((PART, BLK))
        if near == 0:
            left_out[TILE:, :] = jnp.where(keep_low, top, swap_halves(bottom))
        else:
            left_out[TILE:, :] = jnp.where(keep_low, swap_halves(top), bottom)

    def left_far(outer, near):
        for q in range(3):
            start = q * PART
            end = masked(left, lm, outer, q)
            mid = masked(left, lm, 1, q, slice(near * HALF, (near + 1) * HALF))
            left_out[start : start + PART, :] = jnp.concatenate([end, mid] if near == 0 else [mid, end], 0)

    copies[0].wait()
    copies[1].wait()
    for side in (0, 1):
        pl.when(layer == side)(functools.partial(right_side, 2 * side, side))
    copies[2].wait()
    copies[3].wait()
    for side in (0, 1):
        pl.when((layer == side) & far)(functools.partial(left_far, 2 * side, side))
        pl.when((layer == side) & jnp.logical_not(far))(functools.partial(left_side, 2 * side, side))


def split(value):
    high = value.astype(BF16)
    return high, (value - high.astype(F32)).astype(BF16)


def triple(left, right):
    (lh, ll), (rh, rl) = left, right
    dot = functools.partial(jnp.dot, preferred_element_type=F32)
    return dot(lh, rh) + (dot(lh, rl) + dot(ll, rh))


def join_left(one, two):
    m1, m2 = one[TILE:], two[TILE:]
    keep_low = low_lanes((PART, BLK))
    top = jnp.where(keep_low, m1, swap_halves(m2))
    bottom = jnp.where(keep_low, swap_halves(m1), m2)
    return jnp.concatenate([one[:TILE], two[:TILE], jnp.concatenate([top, bottom], 0)], 1)


def join_right(one, two):
    return jnp.concatenate([one[:BLK], two[:BLK], one[BLK:], two[BLK:]], 0)


def along(core):
    return 1 - 2 * core


def panel_index(place, k):
    col, core = place[1], lax.rem(k, 2)
    hops = lax.rem((col // 4 - k // 4) * along(core) + 4, 4)
    return core == lax.rem(col, 2), hops, lax.bitwise_xor(lax.rem(k // 2, 2), lax.rem(col // 2, 2))


def tile_at(place, step):
    z, core = place[0], lax.rem(place[1], 2)
    return lax.rem(z + (2 * core - 1) * step + 16, 16)


def fill_left(place, same, other, one, two, lh, ll, column):
    mine1, y1, x1 = panel_index(place, one)
    mine2, y2, x2 = panel_index(place, one if two is None else two)
    span = slice(column, column + TILE)

    def put(panel1, panel2):
        first = panel1[y1, x1]
        second = jnp.zeros_like(first) if two is None else panel2[y2, x2]
        lh[:, span], ll[:, span] = split(join_left(first, second))

    for is1 in (True, False):
        for is2 in (True, False):
            pl.when((mine1 == is1) & (mine2 == is2))(
                functools.partial(put, same if is1 else other, same if is2 else other)
            )


def fill_right(one, two, rh, rl, row, lane=0):
    rows, lanes = slice(row, row + TILE), slice(lane, lane + TILE)
    rh[rows, lanes], rl[rows, lanes] = split(join_right(one, two))


def fill_rights(place, tiles, rh, rl):
    core = lax.rem(place[1], 2)
    for start in range(0, len(tiles), 2):
        one = tiles[start][...]
        if start == 0:
            one = jnp.where(core == 0, one, jnp.zeros_like(one))
        two = tiles[start + 1][...] if start + 1 < len(tiles) else jnp.zeros_like(one)
        fill_right(one, two, rh, rl, start * PART)


def spare_kernel(steps, same, other, *refs):
    place = coordinates()
    tiles, (spare, lh, ll, far, late_h, late_l, rh, rl) = refs[:steps], refs[steps:]
    for start in range(0, steps, 2):
        two = tile_at(place, start + 1) if start + 1 < steps else None
        fill_left(place, same, other, tile_at(place, start), two, lh, ll, start * PART)
    fill_rights(place, tiles, rh, rl)
    spare[...] = triple((lh[...], ll[...]), (rh[...], rl[...]))
    for number, step in enumerate((steps, steps + 1)):
        fill_left(place, same, other, tile_at(place, step), tile_at(place, -step), late_h, late_l, number * TILE)
    here, y, x = panel_index(place, lax.rem(place[0] + 8, 16))

    @pl.when(here)
    def _():
        far[...] = same[y, x]

    @pl.when(jnp.logical_not(here))
    def _():
        far[...] = other[y, x]


def main_kernel(steps, lh, ll, *refs):
    place = coordinates()
    tiles, (total, rh, rl) = refs[:steps], refs[steps:]
    fill_rights(place, tiles, rh, rl)
    total[...] = triple((lh[...], ll[...]), (rh[...], rl[...]))


def near_kernel(total, spare, late_h, late_l, one, two, three, four, own, away, rh, rl):
    place = coordinates()
    fill_right(one[...], two[...], rh, rl, 0)
    fill_right(three[...], four[...], rh, rl, TILE)
    value = total[...] + spare[...] + triple((late_h[...], late_l[...]), (rh[...], rl[...]))
    layer = place[2]

    @pl.when(layer == 0)
    def _():
        own[...] = value[:PART]
        away[...] = value[PART:]

    @pl.when(layer == 1)
    def _():
        own[...] = value[PART:]
        away[...] = value[:PART]


def last_kernel(keep, own, came, far, right_own, right_other, out):
    place = coordinates()
    layer = place[2]
    first = layer == 0
    mine, other = right_own[...], right_other[...]
    low, high = jnp.where(first, mine, other), jnp.where(first, other, mine)
    right = jnp.concatenate([low, high[BLK:], high[:BLK]], 0)
    left = jnp.concatenate([far[:PART], far[PART : 2 * PART], far[2 * PART :]], 1)
    value = own[...] + came[...] + triple(split(left), split(right))
    row = lax.broadcasted_iota(jnp.int32, (PART, BLK), 0) + layer * PART
    centre = (row >= BLK) & (row < 2 * BLK)
    for q in range(3):
        lanes = slice(q * BLK, (q + 1) * BLK)
        ends = jnp.where(first, keep[0:1, q : q + 1], keep[2:3, q : q + 1]).astype(F32)
        scale = jnp.where(centre, keep[1:2, q : q + 1].astype(F32), ends)
        out[:, lanes] = value[:, lanes] * scale


def move(value, axes, target):
    sizes = [lax.axis_size(axis) for axis in axes]
    flat = lambda at: functools.reduce(lambda total, pair: total * pair[1] + pair[0] % pair[1], zip(at, sizes), 0)
    points = list(itertools.product(*map(range, sizes)))
    return lax.ppermute(value, axes, [(flat(at), flat(target(*at))) for at in points])


def onward(value):
    return move(value, ("row", "col"), lambda z, c: (z + along(c % 2), c))


def after(value, *earlier):
    return lax.optimization_barrier((value, *earlier))[0]


def shards(left_values, left_mask, right_values, right_mask, keep_mask):
    count = lax.axis_size("row")
    packed = jax.ShapeDtypeStruct((TILE + PART, BLK), F32)
    half = jax.ShapeDtypeStruct((PART, TILE), F32)
    whole = jax.ShapeDtypeStruct((TILE, TILE), F32)
    mask = pltpu.VMEM((3, 3), jnp.int32)

    left, right = call(
        prep_kernel, (packed, half), [ANY] * 4,
        [mask, mask, pltpu.VMEM((TILE, TILE), F32), pltpu.VMEM((TILE, TILE), F32), pltpu.SemaphoreType.DMA((4,))],
        nbytes=2**21, limit=60,
    )(left_mask, right_mask, left_values, right_values)

    with jax.named_scope("right_core"):
        right_other = move(right, ("col",), lambda c: (c ^ 1,))
    with jax.named_scope("left_x"):
        left_x = move(left, ("col",), lambda c: (c ^ 2,))
    pair = jnp.stack([left, left_x])

    steps = count // 2 - 1
    mine, others = [right], [right_other]
    one, two = right, right_other
    for step in range(1, steps + 1):
        if step == 3:
            one, two = after(one, pair), after(two, pair)
        with jax.named_scope(f"own{step}"):
            one = onward(one)
        with jax.named_scope(f"other{step}"):
            if step < steps:
                two = onward(two)
            else:
                two = move(two, ("row", "col"), lambda z, c: (z + along(c % 2), c ^ 1))
        mine.append(one)
        others.append(two)
        if step == 1:
            with jax.named_scope("left_y1"):
                left_y1 = move(after(pair, one, two), ("col",), lambda c: (c + 4 * along(c % 2),))
        if step == 2:
            with jax.named_scope("left_y3"):
                left_y3 = move(after(pair, one, two), ("col",), lambda c: (c - 4 * along(c % 2),))
        if step == 3:
            with jax.named_scope("left_y2"):
                left_y2 = move(after(left_y1, one), ("col",), lambda c: (c + 4 * along(c % 2),))
        if step == 5:
            with jax.named_scope("left_core"):
                same = after(jnp.stack([pair, left_y1, left_y2, left_y3]), one, two)
                other = move(same, ("col",), lambda c: (c ^ 1,))

    with jax.named_scope("crossed"):
        crossed = move(others[steps - 1], ("col",), lambda c: (c ^ 1,))
    early = steps - 1
    span = early * PART
    part = jax.ShapeDtypeStruct((TILE, 2 * TILE), BF16)
    lefts = jax.ShapeDtypeStruct((TILE, span), BF16)
    rights = [pltpu.VMEM((span, TILE), BF16)] * 2
    spare, left_h, left_l, far, late_h, late_l = call(
        functools.partial(spare_kernel, early), (whole, lefts, lefts, packed, part, part), [VMEM] * (2 + early),
        rights, flops=6 * span * TILE**2, nbytes=6 * 2**20,
    )(same, other, *others[:early])
    total = call(
        functools.partial(main_kernel, early), whole, [VMEM] * (2 + early), rights,
        flops=6 * span * TILE**2, nbytes=4 * 2**20,
    )(left_h, left_l, *mine[:early])
    with jax.named_scope("spare"):
        spare = move(spare, ("col",), lambda c: (c ^ 1,))
    rights = pltpu.VMEM((2 * TILE, TILE), BF16)
    own, away = call(
        near_kernel, (half, half), [VMEM] * 8, [rights, rights], flops=12 * TILE**3, nbytes=2**21
    )(total, spare, late_h, late_l, mine[early], crossed, one, two)
    with jax.named_scope("away"):
        came = move(away, ("layer",), lambda l: (1 - l,))
    one, two = after(one, total), after(two, total)
    with jax.named_scope("far_own"):
        far_own = onward(one)
    with jax.named_scope("far_other"):
        far_other = move(two, ("row", "col", "layer"), lambda z, c, l: (z - along(c % 2), c, 1 - l))
    return call(last_kernel, half, [VMEM] * 6, flops=6 * PART * TILE * TILE, nbytes=2**20)(
        keep_mask, own, came, far, far_own, far_other
    )


def solution(mesh):
    specs = (P("row", "col"),) * 5
    return jax.shard_map(shards, mesh=mesh, in_specs=specs, out_specs=P(("row", "layer"), "col"), check_vma=False)
```

```python
import functools
import itertools

import jax
import jax.numpy as jnp
from jax import lax
from jax.experimental import pallas as pl
from jax.experimental.pallas import tpu as pltpu
from jax.sharding import PartitionSpec as P

BLK = 128
HALF = 64
TILE = 3 * BLK
PART = TILE // 2
F32 = jnp.float32
BF16 = jnp.bfloat16
VMEM = pl.BlockSpec(memory_space=pltpu.VMEM)
ANY = pl.BlockSpec(memory_space=pl.ANY)


def call(kernel, out_shapes, in_specs, scratch=(), flops=0, nbytes=0, limit=20):
    return pl.pallas_call(
        kernel,
        out_shape=out_shapes,
        in_specs=in_specs,
        out_specs=jax.tree.map(lambda _: VMEM, out_shapes),
        scratch_shapes=scratch,
        compiler_params=pltpu.CompilerParams(vmem_limit_bytes=limit * 2**20),
        cost_estimate=pl.CostEstimate(flops=flops, bytes_accessed=nbytes, transcendentals=0),
    )


def swap_halves(value):
    return pltpu.roll(value, HALF, 1)


def low_lanes(shape):
    return lax.broadcasted_iota(jnp.int32, shape, 1) < HALF


def fetch(pairs, sems):
    copies = [pltpu.make_async_copy(src, dst, sems.at[i]) for i, (src, dst) in enumerate(pairs)]
    for copy in copies:
        copy.start()
    return copies


def masked(values, mask, p, q, rows=slice(0, BLK)):
    block = values[p * BLK + rows.start : p * BLK + rows.stop, q * BLK : (q + 1) * BLK]
    return block * mask[p : p + 1, q : q + 1].astype(F32)


def coordinates():
    return lax.axis_index("row"), lax.axis_index("col"), lax.axis_index("layer")


def prep_kernel(lm_in, rm_in, left_in, right_in, left_out, right_out, lm, rm, left, right, sems):
    place = coordinates()
    z, col, layer = place[0], place[1], place[2]
    copies = fetch(((rm_in, rm), (right_in, right), (lm_in, lm), (left_in, left)), sems)
    far = lax.rem(z + 8, 16) == col

    def right_side(outer, near):
        rows = slice(near * HALF, (near + 1) * HALF)
        for q in range(3):
            lanes = slice(q * BLK, (q + 1) * BLK)
            right_out[:BLK, lanes] = masked(right, rm, outer, q)
            right_out[BLK:, lanes] = masked(right, rm, 1, q, rows)

    def left_side(outer, near):
        for p in range(3):
            left_out[p * BLK : (p + 1) * BLK, :] = masked(left, lm, p, outer)
        middle = jnp.concatenate([masked(left, lm, p, 1) for p in range(3)], 0)
        top, bottom = middle[:PART], middle[PART:]
        keep_low = low_lanes((PART, BLK))
        if near == 0:
            left_out[TILE:, :] = jnp.where(keep_low, top, swap_halves(bottom))
        else:
            left_out[TILE:, :] = jnp.where(keep_low, swap_halves(top), bottom)

    def left_far(outer, near):
        for q in range(3):
            start = q * PART
            end = masked(left, lm, outer, q)
            mid = masked(left, lm, 1, q, slice(near * HALF, (near + 1) * HALF))
            left_out[start : start + PART, :] = jnp.concatenate([end, mid] if near == 0 else [mid, end], 0)

    copies[0].wait()
    copies[1].wait()
    for side in (0, 1):
        pl.when(layer == side)(functools.partial(right_side, 2 * side, side))
    copies[2].wait()
    copies[3].wait()
    for side in (0, 1):
        pl.when((layer == side) & far)(functools.partial(left_far, 2 * side, side))
        pl.when((layer == side) & jnp.logical_not(far))(functools.partial(left_side, 2 * side, side))


def split(value):
    high = value.astype(BF16)
    return high, (value - high.astype(F32)).astype(BF16)


def triple(left, right):
    (lh, ll), (rh, rl) = left, right
    dot = functools.partial(jnp.dot, preferred_element_type=F32)
    return dot(lh, rh) + (dot(lh, rl) + dot(ll, rh))


def join_left(one, two):
    m1, m2 = one[TILE:], two[TILE:]
    keep_low = low_lanes((PART, BLK))
    top = jnp.where(keep_low, m1, swap_halves(m2))
    bottom = jnp.where(keep_low, swap_halves(m1), m2)
    return jnp.concatenate([one[:TILE], two[:TILE], jnp.concatenate([top, bottom], 0)], 1)


def join_right(one, two):
    return jnp.concatenate([one[:BLK], two[:BLK], one[BLK:], two[BLK:]], 0)


def along(core):
    return 1 - 2 * core


def panel_index(place, k):
    col, core = place[1], lax.rem(k, 2)
    hops = lax.rem((col // 4 - k // 4) * along(core) + 4, 4)
    return core == lax.rem(col, 2), hops, lax.bitwise_xor(lax.rem(k // 2, 2), lax.rem(col // 2, 2))


def tile_at(place, step):
    z, core = place[0], lax.rem(place[1], 2)
    return lax.rem(z + (2 * core - 1) * step + 16, 16)


def fill_left(place, same, other, one, two, lh, ll, column):
    mine1, y1, x1 = panel_index(place, one)
    mine2, y2, x2 = panel_index(place, one if two is None else two)
    span = slice(column, column + TILE)

    def put(panel1, panel2):
        first = panel1[y1, x1]
        second = jnp.zeros_like(first) if two is None else panel2[y2, x2]
        lh[:, span], ll[:, span] = split(join_left(first, second))

    for is1 in (True, False):
        for is2 in (True, False):
            pl.when((mine1 == is1) & (mine2 == is2))(
                functools.partial(put, same if is1 else other, same if is2 else other)
            )


def fill_right(one, two, rh, rl, row, lane=0):
    rows, lanes = slice(row, row + TILE), slice(lane, lane + TILE)
    rh[rows, lanes], rl[rows, lanes] = split(join_right(one, two))


def fill_rights(place, tiles, rh, rl):
    core = lax.rem(place[1], 2)
    for start in range(0, len(tiles), 2):
        one = tiles[start][...]
        if start == 0:
            one = jnp.where(core == 0, one, jnp.zeros_like(one))
        two = tiles[start + 1][...] if start + 1 < len(tiles) else jnp.zeros_like(one)
        fill_right(one, two, rh, rl, start * PART)


def spare_kernel(steps, same, other, *refs):
    place = coordinates()
    tiles, (spare, lh, ll, far, late_h, late_l, rh, rl) = refs[:steps], refs[steps:]
    for start in range(0, steps, 2):
        two = tile_at(place, start + 1) if start + 1 < steps else None
        fill_left(place, same, other, tile_at(place, start), two, lh, ll, start * PART)
    fill_rights(place, tiles, rh, rl)
    spare[...] = triple((lh[...], ll[...]), (rh[...], rl[...]))
    for number, step in enumerate((steps, steps + 1)):
        fill_left(place, same, other, tile_at(place, step), tile_at(place, -step), late_h, late_l, number * TILE)
    here, y, x = panel_index(place, lax.rem(place[0] + 8, 16))

    @pl.when(here)
    def _():
        far[...] = same[y, x]

    @pl.when(jnp.logical_not(here))
    def _():
        far[...] = other[y, x]


def main_kernel(steps, lh, ll, *refs):
    place = coordinates()
    tiles, (total, rh, rl) = refs[:steps], refs[steps:]
    fill_rights(place, tiles, rh, rl)
    total[...] = triple((lh[...], ll[...]), (rh[...], rl[...]))


def near_kernel(total, spare, late_h, late_l, one, two, three, four, own, away, rh, rl):
    place = coordinates()
    fill_right(one[...], two[...], rh, rl, 0)
    fill_right(three[...], four[...], rh, rl, TILE)
    value = total[...] + spare[...] + triple((late_h[...], late_l[...]), (rh[...], rl[...]))
    layer = place[2]

    @pl.when(layer == 0)
    def _():
        own[...] = value[:PART]
        away[...] = value[PART:]

    @pl.when(layer == 1)
    def _():
        own[...] = value[PART:]
        away[...] = value[:PART]


def last_kernel(keep, own, came, far, right_own, right_other, out):
    place = coordinates()
    layer = place[2]
    first = layer == 0
    mine, other = right_own[...], right_other[...]
    low, high = jnp.where(first, mine, other), jnp.where(first, other, mine)
    right = jnp.concatenate([low, high[BLK:], high[:BLK]], 0)
    left = jnp.concatenate([far[:PART], far[PART : 2 * PART], far[2 * PART :]], 1)
    value = own[...] + came[...] + triple(split(left), split(right))
    row = lax.broadcasted_iota(jnp.int32, (PART, BLK), 0) + layer * PART
    centre = (row >= BLK) & (row < 2 * BLK)
    for q in range(3):
        lanes = slice(q * BLK, (q + 1) * BLK)
        ends = jnp.where(first, keep[0:1, q : q + 1], keep[2:3, q : q + 1]).astype(F32)
        scale = jnp.where(centre, keep[1:2, q : q + 1].astype(F32), ends)
        out[:, lanes] = value[:, lanes] * scale


def move(value, axes, target):
    sizes = [lax.axis_size(axis) for axis in axes]
    flat = lambda at: functools.reduce(lambda total, pair: total * pair[1] + pair[0] % pair[1], zip(at, sizes), 0)
    points = list(itertools.product(*map(range, sizes)))
    return lax.ppermute(value, axes, [(flat(at), flat(target(*at))) for at in points])


def onward(value):
    return move(value, ("row", "col"), lambda z, c: (z + along(c % 2), c))


def after(value, *earlier):
    return lax.optimization_barrier((value, *earlier))[0]


def shards(left_values, left_mask, right_values, right_mask, keep_mask):
    count = lax.axis_size("row")
    packed = jax.ShapeDtypeStruct((TILE + PART, BLK), F32)
    half = jax.ShapeDtypeStruct((PART, TILE), F32)
    whole = jax.ShapeDtypeStruct((TILE, TILE), F32)
    mask = pltpu.VMEM((3, 3), jnp.int32)

    left, right = call(
        prep_kernel, (packed, half), [ANY] * 4,
        [mask, mask, pltpu.VMEM((TILE, TILE), F32), pltpu.VMEM((TILE, TILE), F32), pltpu.SemaphoreType.DMA((4,))],
        nbytes=2**21, limit=60,
    )(left_mask, right_mask, left_values, right_values)

    with jax.named_scope("right_core"):
        right_other = move(right, ("col",), lambda c: (c ^ 1,))
    with jax.named_scope("left_x"):
        left_x = move(left, ("col",), lambda c: (c ^ 2,))
    pair = jnp.stack([left, left_x])

    steps = count // 2 - 1
    mine, others = [right], [right_other]
    one, two = right, right_other
    for step in range(1, steps + 1):
        if step == 3:
            one, two = after(one, pair), after(two, pair)
        with jax.named_scope(f"own{step}"):
            one = onward(one)
        with jax.named_scope(f"other{step}"):
            if step < steps:
                two = onward(two)
            else:
                two = move(two, ("row", "col"), lambda z, c: (z + along(c % 2), c ^ 1))
        mine.append(one)
        others.append(two)
        if step == 1:
            with jax.named_scope("left_y1"):
                left_y1 = move(after(pair, one, two), ("col",), lambda c: (c + 4 * along(c % 2),))
        if step == 2:
            with jax.named_scope("left_y3"):
                left_y3 = move(after(pair, one, two), ("col",), lambda c: (c - 4 * along(c % 2),))
        if step == 3:
            with jax.named_scope("left_y2"):
                left_y2 = move(after(left_y1, one), ("col",), lambda c: (c + 4 * along(c % 2),))
        if step == 5:
            with jax.named_scope("left_core"):
                same = after(jnp.stack([pair, left_y1, left_y2, left_y3]), one, two)
                other = move(same, ("col",), lambda c: (c ^ 1,))

    with jax.named_scope("crossed"):
        crossed = move(others[steps - 1], ("col",), lambda c: (c ^ 1,))
    early = steps - 1
    span = early * PART
    part = jax.ShapeDtypeStruct((TILE, 2 * TILE), BF16)
    lefts = jax.ShapeDtypeStruct((TILE, span), BF16)
    rights = [pltpu.VMEM((span, TILE), BF16)] * 2
    spare, left_h, left_l, far, late_h, late_l = call(
        functools.partial(spare_kernel, early), (whole, lefts, lefts, packed, part, part), [VMEM] * (2 + early),
        rights, flops=6 * span * TILE**2, nbytes=6 * 2**20,
    )(same, other, *others[:early])
    total = call(
        functools.partial(main_kernel, early), whole, [VMEM] * (2 + early), rights,
        flops=6 * span * TILE**2, nbytes=4 * 2**20,
    )(left_h, left_l, *mine[:early])
    with jax.named_scope("spare"):
        spare = move(spare, ("col",), lambda c: (c ^ 1,))
    rights = pltpu.VMEM((2 * TILE, TILE), BF16)
    own, away = call(
        near_kernel, (half, half), [VMEM] * 8, [rights, rights], flops=12 * TILE**3, nbytes=2**21
    )(total, spare, late_h, late_l, mine[early], crossed, one, two)
    with jax.named_scope("away"):
        came = move(away, ("layer",), lambda l: (1 - l,))
    with jax.named_scope("far_own"):
        far_own = onward(one)
    with jax.named_scope("far_other"):
        far_other = move(two, ("row", "col", "layer"), lambda z, c, l: (z - along(c % 2), c, 1 - l))
    return call(last_kernel, half, [VMEM] * 6, flops=6 * PART * TILE * TILE, nbytes=2**20)(
        keep_mask, own, came, far, far_own, far_other
    )


def solution(mesh):
    specs = (P("row", "col"),) * 5
    return jax.shard_map(shards, mesh=mesh, in_specs=specs, out_specs=P(("row", "layer"), "col"), check_vma=False)
```

```python
import functools
import itertools

import jax
import jax.numpy as jnp
from jax import lax
from jax.experimental import pallas as pl
from jax.experimental.pallas import tpu as pltpu
from jax.sharding import PartitionSpec as P

BLK = 128
HALF = 64
TILE = 3 * BLK
PART = TILE // 2
F32 = jnp.float32
BF16 = jnp.bfloat16
VMEM = pl.BlockSpec(memory_space=pltpu.VMEM)
ANY = pl.BlockSpec(memory_space=pl.ANY)


def call(kernel, out_shapes, in_specs, scratch=(), flops=0, nbytes=0, limit=20):
    return pl.pallas_call(
        kernel,
        out_shape=out_shapes,
        in_specs=in_specs,
        out_specs=jax.tree.map(lambda _: VMEM, out_shapes),
        scratch_shapes=scratch,
        compiler_params=pltpu.CompilerParams(vmem_limit_bytes=limit * 2**20),
        cost_estimate=pl.CostEstimate(flops=flops, bytes_accessed=nbytes, transcendentals=0),
    )


def swap_halves(value):
    return pltpu.roll(value, HALF, 1)


def low_lanes(shape):
    return lax.broadcasted_iota(jnp.int32, shape, 1) < HALF


def fetch(pairs, sems):
    copies = [pltpu.make_async_copy(src, dst, sems.at[i]) for i, (src, dst) in enumerate(pairs)]
    for copy in copies:
        copy.start()
    return copies


def masked(values, mask, p, q, rows=slice(0, BLK)):
    block = values[p * BLK + rows.start : p * BLK + rows.stop, q * BLK : (q + 1) * BLK]
    return block * mask[p : p + 1, q : q + 1].astype(F32)


def coordinates():
    return lax.axis_index("row"), lax.axis_index("col"), lax.axis_index("layer")


def prep_kernel(lm_in, rm_in, left_in, right_in, left_out, right_out, lm, rm, left, right, sems):
    place = coordinates()
    z, col, layer = place[0], place[1], place[2]
    copies = fetch(((rm_in, rm), (right_in, right), (lm_in, lm), (left_in, left)), sems)
    far = lax.rem(z + 8, 16) == col

    def right_side(outer, near):
        rows = slice(near * HALF, (near + 1) * HALF)
        for q in range(3):
            lanes = slice(q * BLK, (q + 1) * BLK)
            right_out[:BLK, lanes] = masked(right, rm, outer, q)
            right_out[BLK:, lanes] = masked(right, rm, 1, q, rows)

    def left_side(outer, near):
        for p in range(3):
            left_out[p * BLK : (p + 1) * BLK, :] = masked(left, lm, p, outer)
        middle = jnp.concatenate([masked(left, lm, p, 1) for p in range(3)], 0)
        top, bottom = middle[:PART], middle[PART:]
        keep_low = low_lanes((PART, BLK))
        if near == 0:
            left_out[TILE:, :] = jnp.where(keep_low, top, swap_halves(bottom))
        else:
            left_out[TILE:, :] = jnp.where(keep_low, swap_halves(top), bottom)

    def left_far(outer, near):
        for q in range(3):
            start = q * PART
            end = masked(left, lm, outer, q)
            mid = masked(left, lm, 1, q, slice(near * HALF, (near + 1) * HALF))
            left_out[start : start + PART, :] = jnp.concatenate([end, mid] if near == 0 else [mid, end], 0)

    copies[0].wait()
    copies[1].wait()
    for side in (0, 1):
        pl.when(layer == side)(functools.partial(right_side, 2 * side, side))
    copies[2].wait()
    copies[3].wait()
    for side in (0, 1):
        pl.when((layer == side) & far)(functools.partial(left_far, 2 * side, side))
        pl.when((layer == side) & jnp.logical_not(far))(functools.partial(left_side, 2 * side, side))


def split(value):
    high = value.astype(BF16)
    return high, (value - high.astype(F32)).astype(BF16)


def triple(left, right):
    (lh, ll), (rh, rl) = left, right
    dot = functools.partial(jnp.dot, preferred_element_type=F32)
    return dot(lh, rh) + (dot(lh, rl) + dot(ll, rh))


def join_left(one, two):
    m1, m2 = one[TILE:], two[TILE:]
    keep_low = low_lanes((PART, BLK))
    top = jnp.where(keep_low, m1, swap_halves(m2))
    bottom = jnp.where(keep_low, swap_halves(m1), m2)
    return jnp.concatenate([one[:TILE], two[:TILE], jnp.concatenate([top, bottom], 0)], 1)


def join_right(one, two):
    return jnp.concatenate([one[:BLK], two[:BLK], one[BLK:], two[BLK:]], 0)


def along(core):
    return 1 - 2 * core


def panel_index(place, k):
    col, core = place[1], lax.rem(k, 2)
    hops = lax.rem((col // 4 - k // 4) * along(core) + 4, 4)
    return core == lax.rem(col, 2), hops, lax.bitwise_xor(lax.rem(k // 2, 2), lax.rem(col // 2, 2))


def tile_at(place, step):
    z, core = place[0], lax.rem(place[1], 2)
    return lax.rem(z + (2 * core - 1) * step + 16, 16)


def fill_left(place, same, other, one, two, lh, ll, column):
    mine1, y1, x1 = panel_index(place, one)
    mine2, y2, x2 = panel_index(place, one if two is None else two)
    span = slice(column, column + TILE)

    def put(panel1, panel2):
        first = panel1[y1, x1]
        second = jnp.zeros_like(first) if two is None else panel2[y2, x2]
        lh[:, span], ll[:, span] = split(join_left(first, second))

    for is1 in (True, False):
        for is2 in (True, False):
            pl.when((mine1 == is1) & (mine2 == is2))(
                functools.partial(put, same if is1 else other, same if is2 else other)
            )


def fill_right(one, two, rh, rl, row, lane=0):
    rows, lanes = slice(row, row + TILE), slice(lane, lane + TILE)
    rh[rows, lanes], rl[rows, lanes] = split(join_right(one, two))


def fill_rights(place, tiles, rh, rl):
    core = lax.rem(place[1], 2)
    for start in range(0, len(tiles), 2):
        one = tiles[start][...]
        if start == 0:
            one = jnp.where(core == 0, one, jnp.zeros_like(one))
        two = tiles[start + 1][...] if start + 1 < len(tiles) else jnp.zeros_like(one)
        fill_right(one, two, rh, rl, start * PART)


def spare_kernel(steps, same, other, *refs):
    place = coordinates()
    tiles, (spare, lh, ll, far, late_h, late_l, rh, rl) = refs[:steps], refs[steps:]
    for start in range(0, steps, 2):
        two = tile_at(place, start + 1) if start + 1 < steps else None
        fill_left(place, same, other, tile_at(place, start), two, lh, ll, start * PART)
    fill_rights(place, tiles, rh, rl)
    spare[...] = triple((lh[...], ll[...]), (rh[...], rl[...]))
    for number, step in enumerate((steps, steps + 1)):
        fill_left(place, same, other, tile_at(place, step), tile_at(place, -step), late_h, late_l, number * TILE)
    here, y, x = panel_index(place, lax.rem(place[0] + 8, 16))

    @pl.when(here)
    def _():
        far[...] = same[y, x]

    @pl.when(jnp.logical_not(here))
    def _():
        far[...] = other[y, x]


def main_kernel(steps, lh, ll, *refs):
    place = coordinates()
    tiles, (total, rh, rl) = refs[:steps], refs[steps:]
    fill_rights(place, tiles, rh, rl)
    total[...] = triple((lh[...], ll[...]), (rh[...], rl[...]))


def near_kernel(total, spare, late_h, late_l, one, two, three, four, own, away, rh, rl):
    place = coordinates()
    fill_right(one[...], two[...], rh, rl, 0)
    fill_right(three[...], four[...], rh, rl, TILE)
    value = total[...] + spare[...] + triple((late_h[...], late_l[...]), (rh[...], rl[...]))
    layer = place[2]

    @pl.when(layer == 0)
    def _():
        own[...] = value[:PART]
        away[...] = value[PART:]

    @pl.when(layer == 1)
    def _():
        own[...] = value[PART:]
        away[...] = value[:PART]


def last_kernel(keep, own, came, far, right_own, right_other, out):
    place = coordinates()
    layer = place[2]
    first = layer == 0
    mine, other = right_own[...], right_other[...]
    low, high = jnp.where(first, mine, other), jnp.where(first, other, mine)
    right = jnp.concatenate([low, high[BLK:], high[:BLK]], 0)
    left = jnp.concatenate([far[:PART], far[PART : 2 * PART], far[2 * PART :]], 1)
    value = own[...] + came[...] + triple(split(left), split(right))
    row = lax.broadcasted_iota(jnp.int32, (PART, BLK), 0) + layer * PART
    centre = (row >= BLK) & (row < 2 * BLK)
    for q in range(3):
        lanes = slice(q * BLK, (q + 1) * BLK)
        ends = jnp.where(first, keep[0:1, q : q + 1], keep[2:3, q : q + 1]).astype(F32)
        scale = jnp.where(centre, keep[1:2, q : q + 1].astype(F32), ends)
        out[:, lanes] = value[:, lanes] * scale


def move(value, axes, target):
    sizes = [lax.axis_size(axis) for axis in axes]
    flat = lambda at: functools.reduce(lambda total, pair: total * pair[1] + pair[0] % pair[1], zip(at, sizes), 0)
    points = list(itertools.product(*map(range, sizes)))
    return lax.ppermute(value, axes, [(flat(at), flat(target(*at))) for at in points])


def onward(value):
    return move(value, ("row", "col"), lambda z, c: (z + along(c % 2), c))


def after(value, *earlier):
    return lax.optimization_barrier((value, *earlier))[0]


def shards(left_values, left_mask, right_values, right_mask, keep_mask):
    count = lax.axis_size("row")
    packed = jax.ShapeDtypeStruct((TILE + PART, BLK), F32)
    half = jax.ShapeDtypeStruct((PART, TILE), F32)
    whole = jax.ShapeDtypeStruct((TILE, TILE), F32)
    mask = pltpu.VMEM((3, 3), jnp.int32)

    left, right = call(
        prep_kernel, (packed, half), [ANY] * 4,
        [mask, mask, pltpu.VMEM((TILE, TILE), F32), pltpu.VMEM((TILE, TILE), F32), pltpu.SemaphoreType.DMA((4,))],
        nbytes=2**21, limit=60,
    )(left_mask, right_mask, left_values, right_values)

    with jax.named_scope("right_core"):
        right_other = move(right, ("col",), lambda c: (c ^ 1,))
    with jax.named_scope("left_x"):
        left_x = move(left, ("col",), lambda c: (c ^ 2,))
    pair = jnp.stack([left, left_x])

    steps = count // 2 - 1
    mine, others = [right], [right_other]
    one, two = right, right_other
    for step in range(1, steps + 1):
        if step == 3:
            one, two = after(one, pair), after(two, pair)
        with jax.named_scope(f"own{step}"):
            one = onward(one)
        with jax.named_scope(f"other{step}"):
            if step < steps:
                two = onward(two)
            else:
                two = move(two, ("row", "col"), lambda z, c: (z + along(c % 2), c ^ 1))
        mine.append(one)
        others.append(two)
        if step == 1:
            with jax.named_scope("left_y1"):
                left_y1 = move(after(pair, one, two), ("col",), lambda c: (c + 4 * along(c % 2),))
        if step == 2:
            with jax.named_scope("left_y3"):
                left_y3 = move(after(pair, one, two), ("col",), lambda c: (c - 4 * along(c % 2),))
        if step == 3:
            with jax.named_scope("left_y2"):
                left_y2 = move(after(left_y1, one), ("col",), lambda c: (c + 4 * along(c % 2),))
        if step == 5:
            with jax.named_scope("left_core"):
                same = after(jnp.stack([pair, left_y1, left_y2, left_y3]), one, two)
                other = move(same, ("col",), lambda c: (c ^ 1,))

    with jax.named_scope("crossed"):
        crossed = move(others[steps - 1], ("col",), lambda c: (c ^ 1,))
    early = steps - 1
    span = early * PART
    part = jax.ShapeDtypeStruct((TILE, 2 * TILE), BF16)
    lefts = jax.ShapeDtypeStruct((TILE, span), BF16)
    rights = [pltpu.VMEM((span, TILE), BF16)] * 2
    spare, left_h, left_l, far, late_h, late_l = call(
        functools.partial(spare_kernel, early), (whole, lefts, lefts, packed, part, part), [VMEM] * (2 + early),
        rights, flops=6 * span * TILE**2, nbytes=6 * 2**20,
    )(same, other, *others[:early])
    total = call(
        functools.partial(main_kernel, early), whole, [VMEM] * (2 + early), rights,
        flops=6 * span * TILE**2, nbytes=4 * 2**20,
    )(left_h, left_l, *mine[:early])
    with jax.named_scope("spare"):
        spare = move(after(spare, others[early]), ("col",), lambda c: (c ^ 1,))
    rights = pltpu.VMEM((2 * TILE, TILE), BF16)
    own, away = call(
        near_kernel, (half, half), [VMEM] * 8, [rights, rights], flops=12 * TILE**3, nbytes=2**21
    )(total, spare, late_h, late_l, mine[early], crossed, one, two)
    with jax.named_scope("away"):
        came = move(away, ("layer",), lambda l: (1 - l,))
    with jax.named_scope("far_own"):
        far_own = onward(one)
    with jax.named_scope("far_other"):
        far_other = move(two, ("row", "col", "layer"), lambda z, c, l: (z - along(c % 2), c, 1 - l))
    return call(last_kernel, half, [VMEM] * 6, flops=6 * PART * TILE * TILE, nbytes=2**20)(
        keep_mask, own, came, far, far_own, far_other
    )


def solution(mesh):
    specs = (P("row", "col"),) * 5
    return jax.shard_map(shards, mesh=mesh, in_specs=specs, out_specs=P(("row", "layer"), "col"), check_vma=False)
```
